32 devices in a mesh: parts: 2 (over y), elem: 4 (over z), comp: 2 (over core), sub: 2 (over x).
Axes of the slice: x: 2, y: 2, z: 4, core: 2. Of those that a mesh axis runs over, the one named last changes fastest.
Arguments:
- field: float32 [2, 4, 64, 64, 128], P('comp', None, ('parts', 'elem'), 'sub'), parts along dimension 2, may hold values from -6 to 6
- register: float32 [2, 4, 64, 64, 128], P('comp', None, ('parts', 'elem'), 'sub'), parts along dimension 2, may hold values from -6 to 6
- advect: float32 [2, 3], replicated, may hold values from -0.5 to 0.5
- mixing: float32 [2, 4, 4], replicated, may hold values from -3 to 3
- drag: float32 [2, 4], replicated, may hold values from 0.5 to 2
- face_elem: int32 [2, 8, 2, 192], P('comp', ('parts', 'elem'), 'sub'), parts along dimension 1, may hold values from 0 to 63
- face_side: int32 [2, 8, 2, 192], P('comp', ('parts', 'elem'), 'sub'), parts along dimension 1, may hold values from 0 to 5
- mortar_code: int32 [2, 8, 2, 192], P('comp', ('parts', 'elem'), 'sub'), parts along dimension 1, may hold values from 0 to 5
- partner_rank: int32 [2, 8, 2, 192, 1], P('comp', ('parts', 'elem'), 'sub'), parts along dimension 1, may hold values from 0 to 3; in each aligned block of 192 rows (0 to 191, 192 to 383, ..., all dimensions but the last counted through in order) at most 96 rows name the same one
- partner_elem: int32 [2, 8, 2, 192], P('comp', ('parts', 'elem'), 'sub'), parts along dimension 1, may hold values from 0 to 63
- partner_side: int32 [2, 8, 2, 192], P('comp', ('parts', 'elem'), 'sub'), parts along dimension 1, may hold values from 0 to 5
- partner_quadrant: int32 [2, 8, 2, 192], P('comp', ('parts', 'elem'), 'sub'), parts along dimension 1, may hold values from 0 to 3
- face_count: int32 [2, 8, 2], P('comp', ('parts', 'elem'), 'sub'), parts along dimension 1, may hold values from 144 to 192, as said below
Outputs:
- new_register: float32 [2, 4, 64, 64, 128], P('comp', None, ('parts', 'elem'), 'sub'), parts along dimension 2
- advanced_field: float32 [2, 4, 64, 64, 128], P('comp', None, ('parts', 'elem'), 'sub'), parts along dimension 2
The draws below stay inside these ranges and needn't reach their ends.
There are 2 independent parts, one for each index of `parts`. The reference program is written for one: setup_inputs(seed, part) draws one part's arguments, and reference() takes and returns one part's arrays. A program takes and returns all parts, laid end to end along the dimension named above; an argument that names none is the same for every part. Nothing has to cross between parts.
Inputs may be any that keep to these rules, and one draw needn't show every extreme that they name: `partner_rank`: in the records of one device, at most 96 name the same partner rank. `face_count`: records of a device at positions at or beyond its count are unused.
All inputs are finite; a program needn't handle non-finite values.
Results may differ from the reference program's by a relative error of at most 0.0003.
Values sent between devices are 32-bit elements; how exact they have to be, the bound alone decides.
No kernel may reach another device: no remote copies, remote signals or barrier semaphores. Data moves between devices by JAX's collectives and lax.ppermute only.
A program may use at most 192 MiB of HBM per device.

```python
import math
import jax
import jax.numpy as jnp
import numpy as np
from jax import lax

P_SIZE = 8
NV = 4
EY = 4
EZ = 16
CAP = 192
ELEMS = 64
LX = 8
LY = 32
NX = 32
NY = 64
NZ = 128
SLOT = 96
N_ELEM = 4
N_SUB = 2


def draw_face_count(key, part):
    key = jax.random.fold_in(key, 11)
    primary, secondary = jax.random.split(key)
    devices_total = 2 * N_ELEM * N_SUB
    counts = jax.random.randint(primary, (devices_total,), 3 * CAP // 4, CAP + 1)
    chosen = jax.random.randint(secondary, (), 0, devices_total)
    counts = jnp.where(jnp.arange(devices_total) == chosen, CAP, counts)
    return counts.reshape(2, N_ELEM, N_SUB).astype(jnp.int32)


def plant(values, rng, smallest, high):
    longest = values.shape.index(max(values.shape))
    spots = []
    for shift in (0, 1):
        where = [jax.random.randint(jax.random.fold_in(rng, axis), (), 0, length) for axis, length in enumerate(values.shape)]
        where[longest] = (where[longest] + shift) % values.shape[longest]
        spots.append(tuple(where))
    return values.at[spots[0]].set(smallest).at[spots[1]].set(high)


def levels(stream_key, extent, cuts, low, top_value):
    gain = 1.0
    for dim, shards_of in cuts:
        heights = jax.random.uniform(jax.random.fold_in(jax.random.fold_in(stream_key, 6), dim), (shards_of,), jnp.float32, low / len(cuts), top_value / len(cuts))
        gain = gain * jnp.repeat(jnp.exp(heights), extent[dim] // shards_of).reshape((-1,) + (1,) * (len(extent) - 1 - dim))
    return gain


def shared_out(own_key, own, number, rows, amount, top, most, slope):
    order = jax.random.permutation(own_key, amount)
    packed, common = load_shares(amount, rows * top, most, slope, True), load_shares(amount, rows * top, most, slope, False)
    places = jnp.arange(amount)

    def named(sizes, turn):
        used = int((sizes > 0).sum())
        fixed = max(1, used // 4)
        shifted = fixed + (places - fixed + turn * (used - fixed)) % max(1, amount - fixed)
        return jnp.zeros((amount,), jnp.int32).at[order[jnp.where(places < fixed, places, shifted)]].set(jnp.asarray(sizes, jnp.int32))

    sizes = jnp.where(number % 4 == 0, named(packed, number // 4), named(common, number - number // 4 - 1))
    mixed = jax.random.permutation(jax.random.fold_in(own, 3), amount)
    donor, receiver = mixed[0:amount // 2 * 2:2], mixed[1:amount // 2 * 2:2]
    margin = jnp.minimum(sizes[donor] - 1, most - sizes[receiver]) // 2
    margin = jnp.where((donor == order[0]) | (receiver == order[0]) | (sizes[receiver] == 0), 0, jnp.maximum(margin, 0))
    shifted = jax.random.randint(jax.random.fold_in(own, 4), (amount // 2,), 0, 1 << 20) % (margin + 1)
    sizes = sizes.at[donor].add(-shifted).at[receiver].add(shifted)
    labels = jnp.searchsorted(jnp.cumsum(sizes), jnp.arange(rows * top), side="right").astype(jnp.int32)
    grid = labels.reshape(top, rows).T
    grid = grid[jax.random.permutation(jax.random.fold_in(own, 1), rows)]
    turn = jax.random.randint(jax.random.fold_in(own, 2), (rows, 1), 0, top)
    return jnp.take_along_axis(grid, (jnp.arange(top)[None, :] + turn) % top, axis=1)


def load_shares(number_of, total, bound, skew, full):
    portions = [(1 << 20) // math.isqrt(standing ** skew) + 1 for standing in range(1, number_of + 1)]
    largest = bound if full else min(bound, max(-(-total // number_of), total * portions[0] // sum(portions)))
    least = 1 if total - largest >= number_of - 1 else 0
    holding, rest = [largest] + [least] * (number_of - 1), total - largest - least * (number_of - 1)
    while rest > 0:
        movable = [i for i in range(1, number_of) if holding[i] < largest] or [i for i in range(1, number_of) if holding[i] < bound]
        mass, remaining = sum([portions[i] for i in movable]), rest
        for i in movable:
            more = min(bound - holding[i], max(1, remaining * portions[i] // mass), rest)
            holding[i] = holding[i] + more
            rest = rest - more
    return np.array(holding)


def bell_draw(own_key, dims, width, reach, cuts=(), kind=jnp.bfloat16):
    factor_of = levels(own_key, dims, cuts, -0.22, 0.18) if cuts else 1.0
    array = jax.random.normal(own_key, dims, jnp.float32) * width * factor_of
    return jnp.minimum(jnp.maximum(array, -reach), reach).astype(kind)


def setup_inputs(seed: int = 0, part: int = 0) -> dict:
    seeds = jax.random.split(jax.random.key(seed), 14)
    part_splits = jax.random.split(jax.random.fold_in(seeds[13], part), 14)
    field = bell_draw(part_splits[0], (2, NV, NX, NY, NZ), 1.0, 6.0, ((0, 2), (2, 4), (3, 2)), jnp.float32)
    register = bell_draw(part_splits[1], (2, NV, NX, NY, NZ), 1.0, 6.0, ((0, 2), (2, 4), (3, 2)), jnp.float32)
    advect = jnp.clip(jax.random.uniform(seeds[2], (2, 3), jnp.float32, -0.5, 0.5), -0.5, 0.5)
    mixing = bell_draw(seeds[3], (2, NV, NV), NV ** -0.5, 3.0, (), jnp.float32)
    drag = jnp.clip(jnp.exp(jax.random.uniform(seeds[4], (2, NV), jnp.float32, math.log(0.5), math.log(2.0))), 0.5, 2.0)
    face_elem = plant(jax.random.randint(part_splits[5], (2, N_ELEM, N_SUB, CAP), 0, ELEMS), jax.random.fold_in(part_splits[5], 1), 0, ELEMS - 1).astype(jnp.int32)
    face_side = plant(jax.random.randint(part_splits[6], (2, N_ELEM, N_SUB, CAP), 0, 6), jax.random.fold_in(part_splits[6], 1), 0, 5).astype(jnp.int32)
    mortar_code = plant(jax.random.randint(part_splits[7], (2, N_ELEM, N_SUB, CAP), 0, 6), jax.random.fold_in(part_splits[7], 1), 0, 5).astype(jnp.int32)
    partner_rank_keys = jax.random.split(jax.random.fold_in(part_splits[8], 1), 2 * N_ELEM * N_SUB * CAP // CAP)
    partner_rank_turns = jax.random.permutation(jax.random.fold_in(part_splits[8], 3), 2 * N_ELEM * N_SUB * CAP // CAP)
    partner_rank = jax.vmap(lambda own, number: shared_out(jax.random.fold_in(part_splits[8], 2), own, number, CAP, N_ELEM, 1, SLOT, 2))(partner_rank_keys, partner_rank_turns).reshape((2, N_ELEM, N_SUB, CAP, 1))
    partner_elem = plant(jax.random.randint(part_splits[9], (2, N_ELEM, N_SUB, CAP), 0, ELEMS), jax.random.fold_in(part_splits[9], 1), 0, ELEMS - 1).astype(jnp.int32)
    partner_side = plant(jax.random.randint(part_splits[10], (2, N_ELEM, N_SUB, CAP), 0, 6), jax.random.fold_in(part_splits[10], 1), 0, 5).astype(jnp.int32)
    partner_quadrant = plant(jax.random.randint(part_splits[11], (2, N_ELEM, N_SUB, CAP), 0, 4), jax.random.fold_in(part_splits[11], 1), 0, 3).astype(jnp.int32)
    face_count = draw_face_count(jax.random.fold_in(jax.random.fold_in(seeds[13], part), 71), part)
    return {"field": field, "register": register, "advect": advect, "mixing": mixing, "drag": drag, "face_elem": face_elem, "face_side": face_side, "mortar_code": mortar_code, "partner_rank": partner_rank, "partner_elem": partner_elem, "partner_side": partner_side, "partner_quadrant": partner_quadrant, "face_count": face_count}


upwind_share = 0.5
register_keep = -0.4178904745
section_weight = 1.7201463215
time_step = 0.05
highest = lax.Precision.HIGHEST


def legendre_values(point, count):
    values = [1.0, point]
    for power in range(2, count):
        values.append(((2 * power - 1) * point * values[power - 1] - (power - 1) * values[power - 2]) / power)
    return values[:count]


def matrix_product(left, right):
    inner_count = len(right)
    columns = len(right[0])
    return [[sum(left[row_pos][middle] * right[middle][column] for middle in range(inner_count)) for column in range(columns)] for row_pos in range(len(left))]


def lagrange_rows(points, targets):
    total = len(points)
    result = []
    for target in targets:
        row_values = []
        for column in range(total):
            product = 1.0
            for other in range(total):
                if other != column:
                    product = product * (target - points[other]) / (points[column] - points[other])
            row_values.append(product)
        result.append(row_values)
    return result


def node_tables(nodes):
    degree = nodes - 1
    guesses = [math.cos(math.pi * position / degree) for position in range(nodes)]
    for sweep in range(100):
        updated = []
        for point in guesses:
            values = legendre_values(point, nodes)
            updated.append(point - (point * values[degree] - values[degree - 1]) / (nodes * values[degree]))
        guesses = updated
    points = sorted(guesses)
    points[0] = -1.0
    points[-1] = 1.0
    modal_basis = [legendre_values(point, nodes) for point in points]
    weights = [2.0 / (degree * nodes * legendre_values(point, nodes)[degree] ** 2) for point in points]
    norms = [2.0 / (2 * power + 1) for power in range(degree)] + [2.0 / degree]
    inverse = [[modal_basis[position][power] * weights[position] / norms[power] for position in range(nodes)] for power in range(nodes)]
    end_weight = 2.0 / (degree * nodes)
    barycentric = []
    for position in range(nodes):
        product = 1.0
        for other in range(nodes):
            if other != position:
                product = product * (points[position] - points[other])
        barycentric.append(1.0 / product)
    derivative = []
    for position in range(nodes):
        row_values = []
        for other in range(nodes):
            if other != position:
                row_values.append((barycentric[other] / barycentric[position]) / (points[position] - points[other]))
            else:
                row_values.append(0.0)
        row_values[position] = -sum(row_values)
        derivative.append(row_values)
    lower_mask = [1.0 if point < 0 else 0.0 for point in points]
    upper_mask = [1.0 if point > 0 else 0.0 for point in points]
    send_table = [inverse,
                  matrix_product(inverse, lagrange_rows(points, [(point - 1.0) / 2.0 for point in points])),
                  matrix_product(inverse, lagrange_rows(points, [(point + 1.0) / 2.0 for point in points]))]
    lower_eval = [[value * lower_mask[position] for value in legendre_values(2.0 * points[position] + 1.0, nodes)] for position in range(nodes)]
    upper_eval = [[value * upper_mask[position] for value in legendre_values(2.0 * points[position] - 1.0, nodes)] for position in range(nodes)]
    receive_table = [modal_basis, lower_eval, upper_eval]
    masks = [[1.0] * nodes, lower_mask, upper_mask]
    return (jnp.asarray(derivative, jnp.float32), float(1.0 / end_weight), jnp.asarray(send_table, jnp.float32),
            jnp.asarray(receive_table, jnp.float32), jnp.asarray(masks, jnp.float32))


def volume_rate(field, derivative, speeds):
    variables, size_x, size_y, size_z = field.shape
    nodes = derivative.shape[0]
    shaped = field.reshape(variables, size_x // nodes, nodes, size_y // nodes, nodes, size_z // nodes, nodes)
    along_x = jnp.einsum('mi,vaibjck->vambjck', derivative, shaped, precision=highest)
    along_y = jnp.einsum('mj,vaibjck->vaibmck', derivative, shaped, precision=highest)
    along_z = jnp.einsum('mk,vaibjck->vaibjcm', derivative, shaped, precision=highest)
    total = speeds[0] * along_x + speeds[1] * along_y + speeds[2] * along_z
    return -total.reshape(field.shape)


def surface_rate(field, neighbours, speeds, end_scale, nodes):
    total = jnp.zeros(field.shape, jnp.float32)
    for axis_pos in range(3):
        before, after = neighbours[axis_pos]
        speed = speeds[axis_pos]
        place = lax.broadcasted_iota(jnp.int32, field.shape, axis_pos + 1) % nodes
        first_node = (place == 0).astype(jnp.float32)
        last_node = (place == nodes - 1).astype(jnp.float32)
        right_flux = 0.5 * speed * (field + after) + 0.5 * upwind_share * jnp.abs(speed) * (field - after)
        left_flux = 0.5 * speed * (before + field) + 0.5 * upwind_share * jnp.abs(speed) * (before - field)
        total = total + end_scale * (first_node * (left_flux - speed * field) - last_node * (right_flux - speed * field))
    return total


def component_rate(field, neighbours, speeds, mixing_here, derivative, end_scale, nodes):
    coupled = jnp.einsum('vw,wxyz->vxyz', mixing_here, field, precision=highest)
    return volume_rate(field, derivative, speeds) + surface_rate(field, neighbours, speeds, end_scale, nodes) + coupled


def face_coordinates(side, nodes):
    shape = side.shape + (nodes, nodes)
    first = lax.broadcasted_iota(jnp.int32, shape, side.ndim)
    second = lax.broadcasted_iota(jnp.int32, shape, side.ndim + 1)
    direction = (side // 2)[..., None, None]
    endpoint = ((side % 2) * (nodes - 1))[..., None, None]
    along_x = jnp.where(direction == 0, endpoint, first)
    along_y = jnp.where(direction == 0, first, jnp.where(direction == 1, endpoint, second))
    along_z = jnp.where(direction == 2, endpoint, second)
    return along_x, along_y, along_z


def node_index(elem, side, base_x, base_y, blocks_y, blocks_z, span_y, span_z, nodes):
    along_x, along_y, along_z = face_coordinates(side, nodes)
    elem_x = elem // (blocks_y * blocks_z)
    elem_y = (elem // blocks_z) % blocks_y
    elem_z = elem % blocks_z
    global_x = (base_x + elem_x * nodes)[..., None, None] + along_x
    global_y = (base_y + elem_y * nodes)[..., None, None] + along_y
    global_z = (elem_z * nodes)[..., None, None] + along_z
    return ((global_x * span_y + global_y) * span_z + global_z).astype(jnp.int32)


def pick(table, index):
    onehot = (index[:, None] == jnp.arange(3, dtype=jnp.int32)[None, :]).astype(jnp.float32)
    return jnp.einsum('ro,o...->r...', onehot, table, precision=highest)


def half_index(code, digit):
    quadrant = jnp.maximum(code - 1, 0)
    half = quadrant // 2 if digit == 0 else quadrant % 2
    return jnp.where(code == 0, 0, 1 + half).astype(jnp.int32)


def project(values, code, send_table):
    first_table = pick(send_table, half_index(code, 0))
    second_table = pick(send_table, half_index(code, 1))
    return jnp.einsum('rka,vrab,rlb->rvkl', first_table, values, second_table, precision=highest)


def evaluate(coefs, own, code, receive_table, masks):
    first_table = pick(receive_table, half_index(code, 0))
    second_table = pick(receive_table, half_index(code, 1))
    first_mask = pick(masks, half_index(code, 0))
    second_mask = pick(masks, half_index(code, 1))
    evaluated = jnp.einsum('rik,rvkl,rjl->vrij', first_table, coefs, second_table, precision=highest)
    return evaluated - first_mask[None, :, :, None] * second_mask[None, :, None, :] * own


def global_pairs(field):
    pairs = []
    for axis_pos in (1, 2, 3):
        padded = jnp.pad(field, [(1, 1) if dim == axis_pos else (0, 0) for dim in range(4)])
        length = padded.shape[axis_pos]
        pairs.append((lax.slice_in_dim(padded, 0, length - 2, axis=axis_pos), lax.slice_in_dim(padded, 2, length, axis=axis_pos)))
    return pairs


def reference(field, register, advect, mixing, drag, face_elem, face_side, mortar_code, partner_rank, partner_elem, partner_side, partner_quadrant, face_count):
    derivative, end_scale, send_table, receive_table, masks = node_tables(P_SIZE)
    flat_rate = []
    flat_field = []
    for source in (0, 1):
        rate = component_rate(field[source], global_pairs(field[source]), advect[source], mixing[source], derivative, end_scale, P_SIZE)
        flat_rate.append(rate.reshape(NV, -1))
        flat_field.append(field[source].reshape(NV, -1))
    grid_shape = (N_ELEM, N_SUB, CAP)
    rank_grid = lax.broadcasted_iota(jnp.int32, grid_shape, 0)
    sub_grid = lax.broadcasted_iota(jnp.int32, grid_shape, 1)
    slot_grid = lax.broadcasted_iota(jnp.int32, grid_shape, 2)
    for source in (0, 1):
        target = 1 - source
        in_use = (slot_grid < face_count[source][:, :, None]).reshape(-1)
        source_index = node_index(face_elem[source], face_side[source], rank_grid * LX, sub_grid * LY, EY, EZ, NY, NZ, P_SIZE).reshape(-1, P_SIZE, P_SIZE)
        values = jnp.take(flat_field[source], source_index, axis=1)
        codes = mortar_code[source]
        send_code = jnp.where((codes >= 1) & (codes <= 4), codes, 0).reshape(-1)
        coefs = project(values, send_code, send_table)
        receive_code = jnp.where(codes == 5, 1 + partner_quadrant[source], 0).reshape(-1)
        target_index = node_index(partner_elem[source], partner_side[source], partner_rank[source][..., 0] * LX, sub_grid * LY, EY, EZ, NY, NZ, P_SIZE).reshape(-1, P_SIZE, P_SIZE)
        own = jnp.take(flat_field[target], target_index, axis=1)
        term = evaluate(coefs, own, receive_code, receive_table, masks)
        scale = drag[target][:, None, None, None] * end_scale * in_use.astype(jnp.float32)[None, :, None, None]
        flat_rate[target] = flat_rate[target].at[:, target_index].add(term * scale)
    rate_all = jnp.stack([flat_rate[0].reshape(NV, NX, NY, NZ), flat_rate[1].reshape(NV, NX, NY, NZ)])
    new_register = register_keep * register + time_step * rate_all
    advanced_field = field + section_weight * new_register
    return new_register, advanced_field
```

```python
import functools
import math

import jax
import jax.numpy as jnp
import ml_dtypes
import numpy as np
from jax import lax
from jax.experimental import pallas as pl
from jax.experimental.pallas import tpu as pltpu
from jax.sharding import PartitionSpec as P

NODES = 8
EY = 4
EZ = 16
FACES = 384
CODES = 8

upwind_share = 0.5
register_keep = -0.4178904745
section_weight = 1.7201463215
time_step = 0.05

f32 = jnp.float32
bf16 = jnp.bfloat16


def legendre_values(point, count):
    values = [1.0, point]
    for power in range(2, count):
        values.append(
            ((2 * power - 1) * point * values[power - 1] - (power - 1) * values[power - 2]) / power
        )
    return values[:count]


def lagrange_rows(points, targets):
    total = len(points)
    result = np.ones((len(targets), total))
    for row, target in enumerate(targets):
        for column in range(total):
            for other in range(total):
                if other != column:
                    result[row, column] *= (target - points[other]) / (
                        points[column] - points[other]
                    )
    return result


@functools.lru_cache
def node_tables(nodes):
    degree = nodes - 1
    guesses = [math.cos(math.pi * position / degree) for position in range(nodes)]
    for sweep in range(100):
        updated = []
        for point in guesses:
            values = legendre_values(point, nodes)
            updated.append(
                point - (point * values[degree] - values[degree - 1]) / (nodes * values[degree])
            )
        guesses = updated
    points = sorted(guesses)
    points[0] = -1.0
    points[-1] = 1.0
    basis = np.array([legendre_values(point, nodes) for point in points])
    inverse = np.linalg.inv(basis)
    barycentric = []
    for position in range(nodes):
        product = 1.0
        for other in range(nodes):
            if other != position:
                product = product * (points[position] - points[other])
        barycentric.append(1.0 / product)
    derivative = np.zeros((nodes, nodes))
    for position in range(nodes):
        for other in range(nodes):
            if other != position:
                derivative[position, other] = (
                    barycentric[other] / barycentric[position] / (points[position] - points[other])
                )
        derivative[position, position] = -derivative[position].sum()
    mask = np.array([[point < 0 for point in points], [point > 0 for point in points]], np.float64)
    fine = [lagrange_rows(points, [(point + shift) / 2.0 for point in points]) for shift in (-1, 1)]
    coarse = []
    for half, shift in ((0, 1.0), (1, -1.0)):
        values = np.array([legendre_values(2.0 * point + shift, nodes) for point in points])
        coarse.append((values * mask[half][:, None]) @ inverse)
    return derivative, degree * nodes / 2.0, fine, coarse


def two_parts(matrix):
    high = matrix.astype(np.float32).astype(ml_dtypes.bfloat16)
    low = (matrix - high.astype(np.float64)).astype(ml_dtypes.bfloat16)
    return high, low


@functools.lru_cache
def face_maps():
    _, _, fine, coarse = node_tables(NODES)
    maps = []
    for tables in (fine, coarse):
        for quadrant in range(4):
            first, second = tables[quadrant // 2], tables[quadrant % 2]
            one = np.kron(second.T, first.T)
            maps.append(np.kron(np.eye(2), one))
    return two_parts(np.concatenate(maps, axis=1))


def split(values):
    high = values.astype(bf16)
    return high, (values - high.astype(f32)).astype(bf16)


def dot(left, right):
    return lax.dot_general(left, right, (((1,), (0,)), ((), ())), preferred_element_type=f32)


def dot_t(left, right):
    return lax.dot_general(left, right, (((1,), (1,)), ((), ())), preferred_element_type=f32)


def iota(shape, dim):
    return lax.broadcasted_iota(jnp.int32, shape, dim)


def one(condition):
    return jnp.where(condition, 1.0, 0.0).astype(bf16)


def twice(matrix):
    return jnp.concatenate([matrix, matrix], axis=0)


def block_transpose(parts):
    parts = list(parts)
    block = iota(parts[0].shape, 1) // 16
    for bit in (1, 2, 4):
        upper = (block & bit) != 0
        for g in range(8):
            if g & bit:
                continue
            low, high = parts[g], parts[g | bit]
            parts[g] = jnp.where(upper, pltpu.roll(high, 16 * bit, 1), low)
            parts[g | bit] = jnp.where(upper, high, pltpu.roll(low, 128 - 16 * bit, 1))
    return parts


def lane_order(inverse):
    row, column = iota((128, 128), 1 if inverse else 0), iota((128, 128), 0 if inverse else 1)
    return one(((row // 8) == (column % 16)) & ((row % 8) == (column // 16)))


def end_lanes(ey, inverse):
    z, lane = iota((128, 128), 1 if inverse else 0), iota((128, 128), 0 if inverse else 1)
    return one(
        (lane // 32 == ey) & (z // 8 == lane % 16) & (z % 8 == (NODES - 1) * ((lane // 16) % 2))
    )


def y_row(ref, y):
    return ref[pl.ds(y, 32, stride=32), :]


def face_number(elem, side):
    direction, end = side >> 1, side & 1
    ey, ez = elem >> 4, elem & 15
    group = jnp.where(direction == 2, 16 + 2 * ey + end, direction * 8 + end * 4 + ey)
    return group, ez


def send_kernel(
    ranks, slots, field, elem, side, code, rank, p_elem, p_side, p_quadrant, count, high, low,
    *outs,
):
    messages, faces_out = outs[:ranks], outs[ranks]
    capacity = elem.shape[1]
    me = lax.axis_index("elem")
    used = iota((1, capacity), 1) < count[0, 0]
    group, ez = face_number(elem[...], side[...])
    codes = code[...]
    map_index = jnp.where(codes == 5, 5 + p_quadrant[...], codes)
    apart = rank[...] - me
    apart = jnp.where(apart < 0, apart + ranks, apart)
    apart = jnp.where(used, apart, 200)
    to_group, to_ez = face_number(p_elem[...], p_side[...])
    kind = jnp.where(used, jnp.where(codes == 5, 2 + p_quadrant[...], 1), 0)
    rows = [group, ez, map_index, apart, to_group, to_ez, kind]
    head = jnp.concatenate(
        [row.astype(f32) for row in rows] + [jnp.zeros((1, capacity), f32)], axis=0
    ).astype(bf16)
    here, there = iota((capacity, capacity), 0), iota((capacity, capacity), 1)
    columns = dot_t(one(here == there), head)
    earlier = (columns[:, 3:4] == apart.astype(f32)) & (here < there)
    position = jnp.sum(jnp.where(earlier, 1.0, 0.0), axis=0, keepdims=True)
    slot = apart * slots + position.astype(jnp.int32)

    order = lane_order(False)
    parts = []
    for kind_of in (0, 1):
        blocks = []
        for end in (0, 1):
            for ey in range(EY):
                if kind_of == 0:
                    blocks += [
                        field[pl.ds(v * 256 + (NODES - 1) * end * 32 + ey * 8, 8), :]
                        for v in range(4)
                    ]
                else:
                    blocks.append(y_row(field, ey * 8 + (NODES - 1) * end))
        stacked_high, stacked_low = split(jnp.concatenate(blocks, axis=0))
        moved = dot(jnp.concatenate([stacked_high, stacked_low], axis=1), twice(order))
        turned = block_transpose([moved[g * 32 : (g + 1) * 32] for g in range(8)])
        parts.append(
            jnp.concatenate(
                [turned[b][v * 8 : (v + 1) * 8] for v in range(4) for b in range(8)], axis=0
            )
        )
    ends = jnp.zeros((256, 128), f32)
    for ey in range(EY):
        lines = [y_row(field, ey * 8 + b) for b in range(8)]
        stacked = jnp.concatenate(
            [lines[b][v * 8 : (v + 1) * 8] for v in range(4) for b in range(8)], axis=0
        )
        stacked_high, stacked_low = split(stacked)
        ends += dot(
            jnp.concatenate([stacked_high, stacked_low], axis=1), twice(end_lanes(ey, False))
        )
    parts.append(ends)
    faces = jnp.concatenate(parts, axis=1)
    faces_out[...] = faces

    faces_high, faces_low = split(faces)
    source = (columns[:, 0:1] * 16.0 + columns[:, 1:2]).astype(jnp.int32)
    picked = one(source == iota((capacity, FACES), 1))
    values = dot_t(picked, faces_high) + dot_t(picked, faces_low)
    which = columns[:, 2:3]
    mapped = []
    for half in range(2):
        part = values[:, half * 128 : (half + 1) * 128]
        part_high, part_low = split(part)
        out = dot(jnp.concatenate([part_high, part_low], axis=1), twice(high[...])) + dot(
            part_high, low[...]
        )
        result = part
        for index in range(CODES):
            result = jnp.where(
                which == float(index + 1), out[:, index * 128 : (index + 1) * 128], result
            )
        mapped.append(result)
    mapped_high, mapped_low = split(jnp.concatenate(mapped, axis=1))
    for k in range(ranks):
        placed = one(iota((slots, capacity), 0) + k * slots == slot)
        messages[k][0:slots, :] = dot(placed, mapped_high) + dot(placed, mapped_low)
        messages[k][slots : slots + 8, :] = jnp.zeros((8, 256), f32)
        messages[k][slots : slots + 8, 0:slots] = dot_t(head, placed)


def local_kernel(field, register, advect, mixing, derivative_y, derivative_z, base):
    comp = lax.axis_index("comp")
    derivative, scale, _, _ = node_tables(NODES)
    left, right, speed = [], [], []
    for d in range(3):
        a = advect[comp, d]
        speed.append(a)
        left.append(scale * (0.5 * a + 0.5 * upwind_share * jnp.abs(a)))
        right.append(scale * (0.5 * upwind_share * jnp.abs(a) - 0.5 * a))

    def both_ways(row, column, node, gain_left, gain_right):
        first, last = node == 0, node == NODES - 1
        out = jnp.where((row == column) & first, -gain_left, 0.0)
        out = jnp.where((row == column) & last, -gain_right, out)
        out = jnp.where((row == column - 1) & first, gain_left, out)
        return jnp.where((row == column + 1) & last, gain_right, out)

    row, column = iota((128, 128), 0), iota((128, 128), 1)
    along_z = both_ways(row, column, column % 8, left[2], right[2]) - speed[2] * derivative_z[...]
    z_high, z_low = split(along_z)
    z_high = twice(z_high)
    row, column = iota((256, 256), 0), iota((256, 256), 1)
    node = row % 8
    across = -speed[0] * derivative_y[...]
    across += jnp.where((row == column) & (node == 0), -left[0], 0.0)
    across += jnp.where((row == column) & (node == NODES - 1), -right[0], 0.0)
    same = (row // 32 == column // 32) & (node == column % 8)
    mixed = jnp.zeros((256, 256), f32)
    for v in range(4):
        for w in range(4):
            mixed = jnp.where(
                ((row // 8) % 4 == v) & ((column // 8) % 4 == w), mixing[comp, v, w], mixed
            )
    across += jnp.where(same, mixed, 0.0)
    across_high, across_low = split(across)

    for ey in range(EY):
        lines = [y_row(field, ey * 8 + j) for j in range(8)]
        stacked = jnp.concatenate(lines, axis=0)
        stacked_high, stacked_low = split(stacked)
        rate = dot(jnp.concatenate([stacked_high, stacked_low], axis=1), z_high)
        rate += dot(stacked_high, z_low)
        pair = dot(across_high, jnp.concatenate([stacked_high, stacked_low], axis=1))
        rate += pair[:, :128] + pair[:, 128:] + dot(across_low, stacked_high)
        along_y = []
        for m in range(8):
            total = float(derivative[m, 0]) * lines[0]
            for j in range(1, 8):
                total += float(derivative[m, j]) * lines[j]
            total = -speed[1] * total
            if m == 0:
                total -= left[1] * lines[0]
                if ey > 0:
                    total += left[1] * y_row(field, ey * 8 - 1)
            if m == NODES - 1:
                total -= right[1] * lines[m]
                if ey < EY - 1:
                    total += right[1] * y_row(field, ey * 8 + 8)
            along_y.append(total)
        rate += jnp.concatenate(along_y, axis=0)
        kept = jnp.concatenate([y_row(register, ey * 8 + j) for j in range(8)], axis=0)
        base[ey * 256 : (ey + 1) * 256, :] = register_keep * kept + time_step * rate


def finish_kernel(ranks, slots, *refs):
    messages = refs[:ranks]
    (base, field, faces, x_before, x_after, y_before, y_after, advect, drag, new, advanced) = refs[
        ranks:
    ]
    comp = lax.axis_index("comp")
    scale = node_tables(NODES)[1]
    total = jnp.zeros((FACES, 256), f32)
    masks = jnp.zeros((16, FACES), f32)
    for k in range(ranks):
        head = messages[k][slots : slots + 8, 0:slots]
        kind = head[6:7]
        target = jnp.where(kind > 0.0, head[4:5] * 16.0 + head[5:6], -1.0).astype(jnp.int32)
        placed = one(iota((FACES, slots), 0) == target)
        values_high, values_low = split(messages[k][0:slots, :])
        total += dot(placed, values_high) + dot(placed, values_low)
        row = iota((16, slots), 0)
        quadrant = ((row % 8) // 4) * 2 + row // 8
        live = (kind == 1.0) | (kind == 2.0 + quadrant.astype(f32))
        masks += dot_t(one(live & (kind > 0.0)), placed)
    total = total.T
    terms = []
    for v in range(4):
        gain = drag[comp, v] * (scale * time_step)
        for b in range(8):
            rows = pl.ds((v * 8 + b) * 8, 8)
            count = masks[0:8] if b < 4 else masks[8:16]
            at = (v * 8 + b) * 8
            terms.append(gain * (total[at : at + 8] - count * faces[rows, :]))
    order = twice(lane_order(True))
    on_x = on_y = None
    for kind_of in (0, 1):
        lanes = slice(kind_of * 128, kind_of * 128 + 128)
        turned = block_transpose(
            [jnp.concatenate([terms[v * 8 + b][:, lanes] for v in range(4)], axis=0) for b in range(8)]
        )
        high, low = split(jnp.concatenate(turned, axis=0))
        moved = dot(jnp.concatenate([high, low], axis=1), order)
        if kind_of == 0:
            on_x = moved
        else:
            on_y = moved
    high, low = split(jnp.concatenate([term[:, 256:384] for term in terms], axis=0))
    ends = jnp.concatenate([high, low], axis=1)
    flux = [jnp.abs(advect[comp, d]) for d in range(2)]
    left = [
        time_step * scale * (0.5 * advect[comp, d] + 0.5 * upwind_share * flux[d]) for d in range(2)
    ]
    right = [
        time_step * scale * (0.5 * upwind_share * flux[d] - 0.5 * advect[comp, d]) for d in range(2)
    ]
    for ey in range(EY):
        on_z = dot(ends, twice(end_lanes(ey, True)))
        for j in range(8):
            y = ey * 8 + j
            rate = base[y * 32 : (y + 1) * 32, :]
            rate += jnp.concatenate(
                [on_z[(v * 8 + j) * 8 : (v * 8 + j) * 8 + 8] for v in range(4)], axis=0
            )
            if j in (0, NODES - 1):
                g = (4 if j else 0) + ey
                rate += on_y[g * 32 : (g + 1) * 32]
            if y == 0:
                rate += left[1] * y_before[...]
            if y == 31:
                rate += right[1] * y_after[...]
            new[pl.ds(y, 32, stride=32), :] = rate
    for end in (0, 1):
        for v in range(4):
            at = v * 256 + (NODES - 1) * end * 32
            rows = pl.ds(at, 32)
            coupled = jnp.concatenate(
                [on_x[((end * 4 + ey) * 4 + v) * 8 : ((end * 4 + ey) * 4 + v) * 8 + 8] for ey in range(EY)],
                axis=0,
            )
            beside = left[0] * x_before[v * 32 : v * 32 + 32, :] if end == 0 else right[0] * x_after[v * 32 : v * 32 + 32, :]
            new[rows, :] = new[rows, :] + coupled + beside
    for at in range(0, 1024, 128):
        rows = pl.ds(at, 128)
        advanced[rows, :] = field[rows, :] + section_weight * new[rows, :]


def along(layer, axis, step):
    devices = lax.axis_size(axis)
    pairs = [(i, i + step) for i in range(devices) if 0 <= i + step < devices]
    return lax.ppermute(layer, axis, pairs)


def on_device(
    field, register, advect, mixing, drag, face_elem, face_side, mortar_code, partner_rank,
    partner_elem, partner_side, partner_quadrant, face_count,
):
    ranks = lax.axis_size("elem")
    capacity = face_elem.shape[-1]
    slots = max(2, 2 * capacity // ranks)
    block = field[0]
    flat = field.reshape(1024, 128)
    x_before = along(block[:, -1], "elem", 1).reshape(128, 128)
    x_after = along(block[:, 0], "elem", -1).reshape(128, 128)
    y_before = along(block[:, :, -1], "sub", 1).reshape(32, 128)
    y_after = along(block[:, :, 0], "sub", -1).reshape(32, 128)

    vmem = pl.BlockSpec(memory_space=pltpu.VMEM)
    smem = pl.BlockSpec(memory_space=pltpu.SMEM)
    row = (1, capacity)
    map_high, map_low = face_maps()
    outs = pl.pallas_call(
        functools.partial(send_kernel, ranks, slots),
        out_shape=[jax.ShapeDtypeStruct((slots + 8, 256), f32)] * ranks
        + [jax.ShapeDtypeStruct((256, FACES), f32)],
        in_specs=[vmem] * 8 + [smem] + [vmem] * 2,
        out_specs=[vmem] * (ranks + 1),
        compiler_params=pltpu.CompilerParams(vmem_limit_bytes=32 << 20),
        cost_estimate=pl.CostEstimate(flops=10**8, bytes_accessed=2 << 20, transcendentals=0),
        name="send_faces",
    )(
        flat, face_elem.reshape(row), face_side.reshape(row), mortar_code.reshape(row),
        partner_rank.reshape(row), partner_elem.reshape(row), partner_side.reshape(row),
        partner_quadrant.reshape(row), face_count.reshape(1, 1), map_high, map_low,
    )
    faces = outs[ranks]
    received = []
    for k in range(ranks):
        pairs = [
            (2 * e + c, 2 * ((e + k) % ranks) + 1 - c) for e in range(ranks) for c in range(2)
        ]
        received.append(lax.ppermute(outs[k], ("elem", "comp"), pairs))

    derivative = node_tables(NODES)[0]
    base = pl.pallas_call(
        local_kernel,
        out_shape=jax.ShapeDtypeStruct((1024, 128), f32),
        in_specs=[vmem, vmem, smem, smem, vmem, vmem],
        out_specs=vmem,
        compiler_params=pltpu.CompilerParams(vmem_limit_bytes=32 << 20),
        cost_estimate=pl.CostEstimate(flops=5 * 10**8, bytes_accessed=4 << 20, transcendentals=0),
        name="local_rate",
    )(
        flat, register.reshape(1024, 128), advect, mixing,
        np.kron(np.eye(32), derivative).astype(np.float32),
        np.kron(np.eye(16), derivative.T).astype(np.float32),
    )
    new, advanced = pl.pallas_call(
        functools.partial(finish_kernel, ranks, slots),
        out_shape=[jax.ShapeDtypeStruct((1024, 128), f32)] * 2,
        in_specs=[vmem] * (ranks + 7) + [smem] * 2,
        out_specs=[vmem] * 2,
        compiler_params=pltpu.CompilerParams(vmem_limit_bytes=32 << 20),
        cost_estimate=pl.CostEstimate(flops=10**8, bytes_accessed=4 << 20, transcendentals=0),
        name="couple_and_finish",
    )(*received, base, flat, faces, x_before, x_after, y_before, y_after, advect, drag)
    return new.reshape(field.shape), advanced.reshape(field.shape)


def solution(mesh):
    block = P("comp", None, ("parts", "elem"), "sub", None)
    records = P("comp", ("parts", "elem"), "sub", None)
    in_specs = (
        block, block, P(), P(), P(), records, records, records,
        P("comp", ("parts", "elem"), "sub", None, None), records, records, records,
        P("comp", ("parts", "elem"), "sub"),
    )
    return jax.shard_map(
        on_device, mesh=mesh, in_specs=in_specs, out_specs=(block, block), check_vma=False
    )
```

```python
import functools
import math

import jax
import jax.numpy as jnp
import numpy as np
from jax import lax
from jax.experimental import pallas as pl
from jax.experimental.pallas import tpu as pltpu
from jax.sharding import PartitionSpec as P

NODES = 8
EY = 4
EZ = 16
FACES = 384
CODES = 8

upwind_share = 0.5
register_keep = -0.4178904745
section_weight = 1.7201463215
time_step = 0.05

f32 = jnp.float32
bf16 = jnp.bfloat16


def legendre_values(point, count):
    values = [1.0, point]
    for power in range(2, count):
        values.append(
            ((2 * power - 1) * point * values[power - 1] - (power - 1) * values[power - 2]) / power
        )
    return values[:count]


def lagrange_rows(points, targets):
    total = len(points)
    result = np.ones((len(targets), total))
    for row, target in enumerate(targets):
        for column in range(total):
            for other in range(total):
                if other != column:
                    result[row, column] *= (target - points[other]) / (
                        points[column] - points[other]
                    )
    return result


@functools.lru_cache
def node_tables(nodes):
    degree = nodes - 1
    guesses = [math.cos(math.pi * position / degree) for position in range(nodes)]
    for sweep in range(100):
        updated = []
        for point in guesses:
            values = legendre_values(point, nodes)
            updated.append(
                point - (point * values[degree] - values[degree - 1]) / (nodes * values[degree])
            )
        guesses = updated
    points = sorted(guesses)
    points[0] = -1.0
    points[-1] = 1.0
    basis = np.array([legendre_values(point, nodes) for point in points])
    inverse = np.linalg.inv(basis)
    barycentric = []
    for position in range(nodes):
        product = 1.0
        for other in range(nodes):
            if other != position:
                product = product * (points[position] - points[other])
        barycentric.append(1.0 / product)
    derivative = np.zeros((nodes, nodes))
    for position in range(nodes):
        for other in range(nodes):
            if other != position:
                derivative[position, other] = (
                    barycentric[other] / barycentric[position] / (points[position] - points[other])
                )
        derivative[position, position] = -derivative[position].sum()
    mask = np.array([[point < 0 for point in points], [point > 0 for point in points]], np.float64)
    fine = [lagrange_rows(points, [(point + shift) / 2.0 for point in points]) for shift in (-1, 1)]
    coarse = []
    for half, shift in ((0, 1.0), (1, -1.0)):
        values = np.array([legendre_values(2.0 * point + shift, nodes) for point in points])
        coarse.append((values * mask[half][:, None]) @ inverse)
    return derivative, degree * nodes / 2.0, fine, coarse


def split(values):
    high = values.astype(bf16)
    return high, (values - high.astype(f32)).astype(bf16)


def dot(left, right):
    return lax.dot_general(left, right, (((1,), (0,)), ((), ())), preferred_element_type=f32)


def dot_t(left, right):
    return lax.dot_general(left, right, (((1,), (1,)), ((), ())), preferred_element_type=f32)


def iota(shape, dim):
    return lax.broadcasted_iota(jnp.int32, shape, dim)


def one(condition):
    return jnp.where(condition, 1.0, 0.0).astype(bf16)


def twice(matrix):
    return jnp.concatenate([matrix, matrix], axis=0)


def block_transpose(parts):
    parts = list(parts)
    block = iota(parts[0].shape, 1) // 16
    for bit in (1, 2, 4):
        upper = (block & bit) != 0
        for g in range(8):
            if g & bit:
                continue
            low, high = parts[g], parts[g | bit]
            parts[g] = jnp.where(upper, pltpu.roll(high, 16 * bit, 1), low)
            parts[g | bit] = jnp.where(upper, high, pltpu.roll(low, 128 - 16 * bit, 1))
    return parts


def lane_order(inverse):
    row, column = iota((128, 128), 1 if inverse else 0), iota((128, 128), 0 if inverse else 1)
    return one(((row // 8) == (column % 16)) & ((row % 8) == (column // 16)))


def end_lanes(ey, inverse):
    z, lane = iota((128, 128), 1 if inverse else 0), iota((128, 128), 0 if inverse else 1)
    return one(
        (lane // 32 == ey) & (z // 8 == lane % 16) & (z % 8 == (NODES - 1) * ((lane // 16) % 2))
    )


def table_tiles(tables, node):
    place = iota((8, 128), 0) * 8 + node
    tiles = [jnp.zeros((8, 128), f32) for _ in tables]
    for i in range(8):
        for j in range(8):
            here = place == i * 8 + j
            tiles = [
                jnp.where(here, float(table[j, i]), tile) for table, tile in zip(tables, tiles)
            ]
    return tiles


def y_row(ref, y):
    return ref[pl.ds(y, 32, stride=32), :]


def face_number(elem, side):
    direction, end = side >> 1, side & 1
    ey, ez = elem >> 4, elem & 15
    group = jnp.where(direction == 2, 16 + 2 * ey + end, direction * 8 + end * 4 + ey)
    return group, ez


def send_order(ranks):
    return sorted(range(ranks), key=lambda k: -min(k, ranks - k))


def plan_kernel(
    ranks, slots, elem, side, code, rank, p_elem, p_side, p_quadrant,
    head_out, columns_out, slot_out, maps_high, maps_low,
):
    capacity = elem.shape[1]
    me = lax.axis_index("elem")
    group, ez = face_number(elem[...], side[...])
    codes = code[...]
    map_index = jnp.where(codes == 5, 5 + p_quadrant[...], codes)
    apart = rank[...] - me
    apart = jnp.where(apart < 0, apart + ranks, apart)
    to_group, to_ez = face_number(p_elem[...], p_side[...])
    kind = jnp.where(codes == 5, 2 + p_quadrant[...], 1)
    rows = [group, ez, map_index, apart, to_group, to_ez, kind]
    head = jnp.concatenate(
        [row.astype(f32) for row in rows] + [jnp.zeros((1, capacity), f32)], axis=0
    )
    head_out[...] = head
    here, there = iota((capacity, capacity), 0), iota((capacity, capacity), 1)
    columns = dot_t(one(here == there), head.astype(bf16))
    columns_out[...] = columns
    earlier = (columns[:, 3:4] == apart.astype(f32)) & (here < there)
    position = jnp.sum(jnp.where(earlier, 1.0, 0.0), axis=0, keepdims=True).astype(jnp.int32)
    slot_out[...] = jnp.where(position < slots, apart * slots + position, -1)

    _, _, fine, coarse = node_tables(NODES)
    lane = iota((8, 128), 1)
    along_a = table_tiles(fine + coarse, lane % 8)
    along_b = table_tiles(fine + coarse, lane // 8 % 8)
    for index in range(CODES):
        first = along_a[index // 4 * 2 + index % 4 // 2]
        second = along_b[index // 4 * 2 + index % 2]
        blocks = []
        for v in range(2):
            kept = jnp.where(lane // 64 == v, first, 0.0)
            blocks += [kept * second[b : b + 1, :] for b in range(8)]
        high, low = split(jnp.concatenate(blocks, axis=0))
        lanes = slice(index * 128, index * 128 + 128)
        maps_high[0:128, lanes] = high
        maps_high[128:256, lanes] = high
        maps_low[:, lanes] = low


def send_kernel(ranks, slots, field, count, planned, columns_in, slot_in, maps_high, maps_low, *outs):
    messages, faces_out, layers = outs[:ranks], outs[ranks], outs[ranks + 1 :]
    capacity = planned.shape[1]
    lines = iota((8, capacity), 0)
    unused = (lines == 6) & (iota((8, capacity), 1) >= count[...])
    head = jnp.where(unused, 0.0, planned[...]).astype(bf16)
    columns, slot = columns_in[...], slot_in[...]
    for v in range(4):
        layers[0][v * 32 : v * 32 + 32, :] = field[v * 256 : v * 256 + 32, :]
        layers[1][v * 32 : v * 32 + 32, :] = field[v * 256 + 224 : v * 256 + 256, :]
    if len(layers) == 3:
        layers[2][...] = jnp.where(lax.axis_index("sub") == 0, y_row(field, 31), y_row(field, 0))
    else:
        layers[2][...] = y_row(field, 0)
        layers[3][...] = y_row(field, 31)

    order = lane_order(False)
    parts = []
    for kind_of in (0, 1):
        blocks = []
        for end in (0, 1):
            for ey in range(EY):
                if kind_of == 0:
                    blocks += [
                        field[pl.ds(v * 256 + (NODES - 1) * end * 32 + ey * 8, 8), :]
                        for v in range(4)
                    ]
                else:
                    blocks.append(y_row(field, ey * 8 + (NODES - 1) * end))
        stacked_high, stacked_low = split(jnp.concatenate(blocks, axis=0))
        moved = dot(jnp.concatenate([stacked_high, stacked_low], axis=1), twice(order))
        turned = block_transpose([moved[g * 32 : (g + 1) * 32] for g in range(8)])
        parts.append(
            jnp.concatenate(
                [turned[b][v * 8 : (v + 1) * 8] for v in range(4) for b in range(8)], axis=0
            )
        )
    ends = jnp.zeros((256, 128), f32)
    for ey in range(EY):
        lines = [y_row(field, ey * 8 + b) for b in range(8)]
        stacked = jnp.concatenate(
            [lines[b][v * 8 : (v + 1) * 8] for v in range(4) for b in range(8)], axis=0
        )
        stacked_high, stacked_low = split(stacked)
        ends += dot(
            jnp.concatenate([stacked_high, stacked_low], axis=1), twice(end_lanes(ey, False))
        )
    parts.append(ends)
    faces = jnp.concatenate(parts, axis=1)
    faces_out[...] = faces

    faces_high, faces_low = split(faces)
    source = (columns[:, 0:1] * 16.0 + columns[:, 1:2]).astype(jnp.int32)
    picked = one(source == iota((capacity, FACES), 1))
    values = dot_t(picked, faces_high) + dot_t(picked, faces_low)
    which = columns[:, 2:3]
    pair = jnp.concatenate([values[:, :128], values[:, 128:]], axis=0)
    pair_high, pair_low = split(pair)
    out = dot(jnp.concatenate([pair_high, pair_low], axis=1), maps_high[...])
    out += dot(pair_high, maps_low[...])
    which = jnp.concatenate([which, which], axis=0)
    for index in range(CODES):
        pair = jnp.where(which == float(index + 1), out[:, index * 128 : (index + 1) * 128], pair)
    mapped = [pair[:capacity], pair[capacity:]]
    mapped_high, mapped_low = split(jnp.concatenate(mapped, axis=1))
    for message, k in zip(messages, send_order(ranks)):
        placed = one(iota((slots, capacity), 0) + k * slots == slot)
        rows = dot(placed, mapped_high) + dot(placed, mapped_low)
        message[0:slots, :] = rows[:, :128]
        message[slots : 2 * slots, :] = rows[:, 128:]
        message[2 * slots : 2 * slots + 8, :] = jnp.zeros((8, 128), f32)
        message[2 * slots : 2 * slots + 8, 0:slots] = dot_t(head, placed)


def local_kernel(
    ranks, field, register, advect, mixing, drag, after, base, gains
):
    comp = lax.axis_index("comp")
    derivative, scale, _, _ = node_tables(NODES)
    left, right, speed = [], [], []
    for d in range(3):
        a = advect[comp, d]
        speed.append(a)
        left.append(scale * (0.5 * a + 0.5 * upwind_share * jnp.abs(a)))
        right.append(scale * (0.5 * upwind_share * jnp.abs(a) - 0.5 * a))

    me, sub, subs = lax.axis_index("elem"), lax.axis_index("sub"), lax.axis_size("sub")
    values = [drag[comp, v] * scale for v in range(4)]
    values.append(jnp.where(me > 0, left[0], 0.0))
    values.append(jnp.where(me < ranks - 1, right[0], 0.0))
    values.append(jnp.where(sub > 0, left[1], 0.0))
    values.append(jnp.where(sub < subs - 1, right[1], 0.0))
    line = iota((8, 128), 0)
    lines = jnp.zeros((8, 128), f32)
    for i, value in enumerate(values):
        lines = jnp.where(line == i, time_step * value, lines)
    gains[...] = lines
    tile_z, tile_y = table_tiles([derivative, derivative.T], iota((8, 128), 1) % 8)

    def both_ways(row, column, node, gain_left, gain_right):
        first, last = node == 0, node == NODES - 1
        out = jnp.where((row == column) & first, -gain_left, 0.0)
        out = jnp.where((row == column) & last, -gain_right, out)
        out = jnp.where((row == column - 1) & first, gain_left, out)
        return jnp.where((row == column + 1) & last, gain_right, out)

    row, column = iota((128, 128), 0), iota((128, 128), 1)
    along_z = both_ways(row, column, column % 8, left[2], right[2]) - speed[2] * jnp.where(
        row // 8 == column // 8, jnp.concatenate([tile_z] * 16, axis=0), 0.0
    )
    z_high, z_low = split(along_z)
    z_high = twice(z_high)
    row, column = iota((256, 256), 0), iota((256, 256), 1)
    node = row % 8
    tile = jnp.concatenate([tile_y] * 2, axis=1)
    across = jnp.where(
        row // 8 == column // 8, -speed[0] * jnp.concatenate([tile] * 32, axis=0), 0.0
    )
    across += jnp.where((row == column) & (node == 0), -left[0], 0.0)
    across += jnp.where((row == column) & (node == NODES - 1), -right[0], 0.0)
    same = (row // 32 == column // 32) & (node == column % 8)
    mixed = jnp.zeros((256, 256), f32)
    for v in range(4):
        for w in range(4):
            mixed = jnp.where(
                ((row // 8) % 4 == v) & ((column // 8) % 4 == w), mixing[comp, v, w], mixed
            )
    across += jnp.where(same, mixed, 0.0)
    across_high, across_low = split(across)

    for ey in range(EY):
        lines = [y_row(field, ey * 8 + j) for j in range(8)]
        stacked = jnp.concatenate(lines, axis=0)
        stacked_high, stacked_low = split(stacked)
        rate = dot(jnp.concatenate([stacked_high, stacked_low], axis=1), z_high)
        rate += dot(stacked_high, z_low)
        pair = dot(across_high, jnp.concatenate([stacked_high, stacked_low], axis=1))
        rate += pair[:, :128] + pair[:, 128:] + dot(across_low, stacked_high)
        along_y = []
        for m in range(8):
            total = float(derivative[m, 0]) * lines[0]
            for j in range(1, 8):
                total += float(derivative[m, j]) * lines[j]
            total = -speed[1] * total
            if m == 0:
                total -= left[1] * lines[0]
                if ey > 0:
                    total += left[1] * y_row(field, ey * 8 - 1)
            if m == NODES - 1:
                total -= right[1] * lines[m]
                if ey < EY - 1:
                    total += right[1] * y_row(field, ey * 8 + 8)
            along_y.append(total)
        rate += jnp.concatenate(along_y, axis=0)
        kept = jnp.concatenate([y_row(register, ey * 8 + j) for j in range(8)], axis=0)
        base[ey * 256 : (ey + 1) * 256, :] = register_keep * kept + time_step * rate


def finish_kernel(ranks, slots, *refs):
    messages = refs[:ranks]
    base, field, faces, x_before, x_after, y_before, y_after, gains = refs[ranks : ranks + 8]
    new_out, advanced_out, new, advanced, left = refs[ranks + 8 :]
    total = jnp.zeros((FACES, 256), f32)
    masks = jnp.zeros((16, FACES), f32)
    for message in messages:
        head = message[2 * slots : 2 * slots + 8, 0:slots]
        kind = head[6:7]
        target = jnp.where(kind > 0.0, head[4:5] * 16.0 + head[5:6], -1.0).astype(jnp.int32)
        both = jnp.concatenate([target, target], axis=1)
        placed = one(iota((FACES, 2 * slots), 0) == both)
        values = jnp.concatenate([message[0:slots, :], message[slots : 2 * slots, :]], axis=1)
        high = values.astype(bf16).astype(f32)
        total += dot(placed, jnp.concatenate([high, values - high], axis=0).astype(bf16))
        row = iota((16, 2 * slots), 0)
        quadrant = ((row % 8) // 4) * 2 + row // 8
        kind = jnp.where(iota((1, 2 * slots), 1) < slots, jnp.concatenate([kind, kind], axis=1), 0.0)
        live = (kind == 1.0) | (kind == 2.0 + quadrant.astype(f32))
        masks += dot_t(one(live & (kind > 0.0)), placed)
    total = total.T
    terms = []
    for v in range(4):
        gain = gains[v : v + 1, 0:1]
        for b in range(8):
            at = (v * 8 + b) * 8
            count = masks[0:8] if b < 4 else masks[8:16]
            terms.append(gain * (total[at : at + 8] - count * faces[at : at + 8, :]))
    turned = []
    for lanes in (slice(0, 128), slice(128, 256)):
        turned += block_transpose(
            [
                jnp.concatenate([terms[v * 8 + b][:, lanes] for v in range(4)], axis=0)
                for b in range(8)
            ]
        )
    high, low = split(jnp.concatenate(turned, axis=0))
    moved = dot(jnp.concatenate([high, low], axis=1), twice(lane_order(True)))
    high, low = split(jnp.concatenate([term[:, 256:384] for term in terms], axis=0))
    ends = jnp.concatenate([end_lanes(ey, True) for ey in range(EY)], axis=1)
    on_z = dot(jnp.concatenate([high, low], axis=1), twice(ends))

    copies = []
    for v in range(4):
        for ey in range(EY):
            for j in range(8):
                y = ey * 8 + j
                at = (v * 8 + j) * 8
                rate = base[y * 32 + v * 8 : y * 32 + v * 8 + 8, :]
                rate += on_z[at : at + 8, ey * 128 : ey * 128 + 128]
                if j in (0, NODES - 1):
                    at = ((8 + (4 if j else 0) + ey) * 4 + v) * 8
                    rate += moved[at : at + 8]
                if y == 0:
                    rate += gains[6:7, :] * y_before[v * 8 : v * 8 + 8, :]
                if y == 31:
                    rate += gains[7:8, :] * y_after[v * 8 : v * 8 + 8, :]
                new[pl.ds(v * 256 + y, 8, stride=32), :] = rate
        for end, beside in ((0, x_before), (1, x_after)):
            at = v * 256 + (NODES - 1) * end * 32
            coupled = jnp.concatenate(
                [
                    moved[((end * 4 + ey) * 4 + v) * 8 : ((end * 4 + ey) * 4 + v) * 8 + 8]
                    for ey in range(EY)
                ],
                axis=0,
            )
            coupled += gains[4 + end : 5 + end, :] * beside[v * 32 : v * 32 + 32, :]
            new[pl.ds(at, 32), :] = new[pl.ds(at, 32), :] + coupled
        rows = pl.ds(v * 256, 256)
        advanced[rows, :] = field[rows, :] + section_weight * new[rows, :]
        for i, (source, place) in enumerate(((new, new_out), (advanced, advanced_out))):
            copies.append(
                pltpu.make_async_copy(source.at[rows], place.at[rows], left.at[v * 2 + i])
            )
            copies[-1].start()
    for copy in copies:
        copy.wait()


def along(layer, axis, step):
    devices = lax.axis_size(axis)
    pairs = [(i, i + step) for i in range(devices) if 0 <= i + step < devices]
    return lax.ppermute(layer, axis, pairs)


def on_device(
    field, register, advect, mixing, drag, face_elem, face_side, mortar_code, partner_rank,
    partner_elem, partner_side, partner_quadrant, face_count,
):
    ranks = lax.axis_size("elem")
    capacity = face_elem.shape[-1]
    slots = max(2, 2 * capacity // ranks)
    subs = lax.axis_size("sub")
    layers = 1 if subs == 2 else 2
    flat = field.reshape(1024, 128)
    vmem = pl.BlockSpec(memory_space=pltpu.VMEM)
    smem = pl.BlockSpec(memory_space=pltpu.SMEM)
    row = (1, capacity)
    plan = pl.pallas_call(
        functools.partial(plan_kernel, ranks, slots),
        out_shape=[
            jax.ShapeDtypeStruct((8, capacity), f32),
            jax.ShapeDtypeStruct((capacity, 8), f32),
            jax.ShapeDtypeStruct(row, jnp.int32),
            jax.ShapeDtypeStruct((256, CODES * 128), bf16),
            jax.ShapeDtypeStruct((128, CODES * 128), bf16),
        ],
        in_specs=[vmem] * 7,
        out_specs=[vmem] * 5,
        compiler_params=pltpu.CompilerParams(vmem_limit_bytes=32 << 20),
        cost_estimate=pl.CostEstimate(flops=10**7, bytes_accessed=1 << 20, transcendentals=0),
        name="plan_records",
    )(
        face_elem.reshape(row), face_side.reshape(row), mortar_code.reshape(row),
        partner_rank.reshape(row), partner_elem.reshape(row), partner_side.reshape(row),
        partner_quadrant.reshape(row),
    )
    outs = pl.pallas_call(
        functools.partial(send_kernel, ranks, slots),
        out_shape=[jax.ShapeDtypeStruct((2 * slots + 8, 128), f32)] * ranks
        + [jax.ShapeDtypeStruct((256, FACES), f32)]
        + [jax.ShapeDtypeStruct((128, 128), f32)] * 2
        + [jax.ShapeDtypeStruct((32, 128), f32)] * layers,
        in_specs=[vmem] * 7,
        out_specs=[vmem] * (ranks + 3 + layers),
        compiler_params=pltpu.CompilerParams(vmem_limit_bytes=32 << 20),
        cost_estimate=pl.CostEstimate(flops=10**8, bytes_accessed=2 << 20, transcendentals=0),
        name="send_faces",
    )(flat, face_count.reshape(1, 1), *plan)
    faces = outs[ranks]
    received = [None] * ranks
    for out, k in zip(outs, send_order(ranks)):
        pairs = [
            (2 * e + c, 2 * ((e + k) % ranks) + 1 - c) for e in range(ranks) for c in range(2)
        ]
        received[k] = lax.ppermute(out, ("elem", "comp"), pairs)

    (x_first, x_last, *y_layers), received[0] = lax.optimization_barrier(
        (outs[ranks + 1 :], received[0])
    )
    x_before = along(x_last, "elem", 1)
    x_after = along(x_first, "elem", -1)
    if layers == 1:
        y_before = y_after = lax.ppermute(y_layers[0], "sub", [(0, 1), (1, 0)])
    else:
        y_before = along(y_layers[1], "sub", 1)
        y_after = along(y_layers[0], "sub", -1)
    base, gains = pl.pallas_call(
        functools.partial(local_kernel, ranks),
        out_shape=[
            jax.ShapeDtypeStruct((1024, 128), f32),
            jax.ShapeDtypeStruct((8, 128), f32),
        ],
        in_specs=[vmem, vmem, smem, smem, smem, pl.BlockSpec(memory_space=pl.ANY)],
        out_specs=[vmem] * 2,
        compiler_params=pltpu.CompilerParams(vmem_limit_bytes=32 << 20),
        cost_estimate=pl.CostEstimate(flops=5 * 10**8, bytes_accessed=4 << 20, transcendentals=0),
        name="local_rate",
    )(
        flat, register.reshape(1024, 128), advect, mixing, drag, received[0],
    )
    new, advanced = pl.pallas_call(
        functools.partial(finish_kernel, ranks, slots),
        out_shape=[jax.ShapeDtypeStruct((1024, 128), f32)] * 2,
        in_specs=[vmem] * (ranks + 8),
        out_specs=[pl.BlockSpec(memory_space=pl.ANY)] * 2,
        scratch_shapes=[pltpu.VMEM((1024, 128), f32)] * 2 + [pltpu.SemaphoreType.DMA((8,))],
        compiler_params=pltpu.CompilerParams(vmem_limit_bytes=32 << 20),
        cost_estimate=pl.CostEstimate(flops=10**8, bytes_accessed=4 << 20, transcendentals=0),
        name="couple_and_finish",
    )(*received, base, flat, faces, x_before, x_after, y_before, y_after, gains)
    return new.reshape(field.shape), advanced.reshape(field.shape)


def solution(mesh):
    block = P("comp", None, ("parts", "elem"), "sub", None)
    records = P("comp", ("parts", "elem"), "sub", None)
    in_specs = (
        block, block, P(), P(), P(), records, records, records,
        P("comp", ("parts", "elem"), "sub", None, None), records, records, records,
        P("comp", ("parts", "elem"), "sub"),
    )
    return jax.shard_map(
        on_device, mesh=mesh, in_specs=in_specs, out_specs=(block, block), check_vma=False
    )
```

```python
import functools
import math

import jax
import jax.numpy as jnp
import numpy as np
from jax import lax
from jax.experimental import pallas as pl
from jax.experimental.pallas import tpu as pltpu
from jax.sharding import PartitionSpec as P

NODES = 8
EY = 4
EZ = 16
FACES = 384
CODES = 8

upwind_share = 0.5
register_keep = -0.4178904745
section_weight = 1.7201463215
time_step = 0.05

f32 = jnp.float32
bf16 = jnp.bfloat16


def legendre_values(point, count):
    values = [1.0, point]
    for power in range(2, count):
        values.append(
            ((2 * power - 1) * point * values[power - 1] - (power - 1) * values[power - 2]) / power
        )
    return values[:count]


def lagrange_rows(points, targets):
    total = len(points)
    result = np.ones((len(targets), total))
    for row, target in enumerate(targets):
        for column in range(total):
            for other in range(total):
                if other != column:
                    result[row, column] *= (target - points[other]) / (
                        points[column] - points[other]
                    )
    return result


@functools.lru_cache
def node_tables(nodes):
    degree = nodes - 1
    guesses = [math.cos(math.pi * position / degree) for position in range(nodes)]
    for sweep in range(100):
        updated = []
        for point in guesses:
            values = legendre_values(point, nodes)
            updated.append(
                point - (point * values[degree] - values[degree - 1]) / (nodes * values[degree])
            )
        guesses = updated
    points = sorted(guesses)
    points[0] = -1.0
    points[-1] = 1.0
    basis = np.array([legendre_values(point, nodes) for point in points])
    inverse = np.linalg.inv(basis)
    barycentric = []
    for position in range(nodes):
        product = 1.0
        for other in range(nodes):
            if other != position:
                product = product * (points[position] - points[other])
        barycentric.append(1.0 / product)
    derivative = np.zeros((nodes, nodes))
    for position in range(nodes):
        for other in range(nodes):
            if other != position:
                derivative[position, other] = (
                    barycentric[other] / barycentric[position] / (points[position] - points[other])
                )
        derivative[position, position] = -derivative[position].sum()
    mask = np.array([[point < 0 for point in points], [point > 0 for point in points]], np.float64)
    fine = [lagrange_rows(points, [(point + shift) / 2.0 for point in points]) for shift in (-1, 1)]
    coarse = []
    for half, shift in ((0, 1.0), (1, -1.0)):
        values = np.array([legendre_values(2.0 * point + shift, nodes) for point in points])
        coarse.append((values * mask[half][:, None]) @ inverse)
    return derivative, degree * nodes / 2.0, fine, coarse


def split(values):
    high = values.astype(bf16)
    return high, (values - high.astype(f32)).astype(bf16)


def dot(left, right):
    return lax.dot_general(left, right, (((1,), (0,)), ((), ())), preferred_element_type=f32)


def dot_t(left, right):
    return lax.dot_general(left, right, (((1,), (1,)), ((), ())), preferred_element_type=f32)


def iota(shape, dim):
    return lax.broadcasted_iota(jnp.int32, shape, dim)


def one(condition):
    return jnp.where(condition, 1.0, 0.0).astype(bf16)


def twice(matrix):
    return jnp.concatenate([matrix, matrix], axis=0)


def block_transpose(parts):
    parts = list(parts)
    block = iota(parts[0].shape, 1) // 16
    for bit in (1, 2, 4):
        upper = (block & bit) != 0
        for g in range(8):
            if g & bit:
                continue
            low, high = parts[g], parts[g | bit]
            parts[g] = jnp.where(upper, pltpu.roll(high, 16 * bit, 1), low)
            parts[g | bit] = jnp.where(upper, high, pltpu.roll(low, 128 - 16 * bit, 1))
    return parts


def lane_order(inverse):
    row, column = iota((128, 128), 1 if inverse else 0), iota((128, 128), 0 if inverse else 1)
    return one(((row // 8) == (column % 16)) & ((row % 8) == (column // 16)))


def end_lanes(ey, inverse):
    z, lane = iota((128, 128), 1 if inverse else 0), iota((128, 128), 0 if inverse else 1)
    return one(
        (lane // 32 == ey) & (z // 8 == lane % 16) & (z % 8 == (NODES - 1) * ((lane // 16) % 2))
    )


def table_tiles(tables, node):
    place = iota((8, 128), 0) * 8 + node
    tiles = [jnp.zeros((8, 128), f32) for _ in tables]
    for i in range(8):
        for j in range(8):
            here = place == i * 8 + j
            tiles = [
                jnp.where(here, float(table[j, i]), tile) for table, tile in zip(tables, tiles)
            ]
    return tiles


def y_row(ref, y):
    return ref[pl.ds(y, 32, stride=32), :]


def face_number(elem, side):
    direction, end = side >> 1, side & 1
    ey, ez = elem >> 4, elem & 15
    group = jnp.where(direction == 2, 16 + 2 * ey + end, direction * 8 + end * 4 + ey)
    return group, ez


def send_order(ranks):
    return list(range(ranks))[::-1]


def neighbour_messages(ranks):
    return [k for k in range(1, ranks) if k & (k + 1) == 0]


def plan_kernel(
    ranks, slots, elem, side, code, rank, p_elem, p_side, p_quadrant,
    head_out, which_out, picked_out, placed_out, maps_high, maps_low,
):
    capacity = elem.shape[1]
    me = lax.axis_index("elem")
    group, ez = face_number(elem[...], side[...])
    codes = code[...]
    map_index = jnp.where(codes == 5, 5 + p_quadrant[...], codes)
    apart = rank[...] ^ me
    to_group, to_ez = face_number(p_elem[...], p_side[...])
    kind = jnp.where(codes == 5, 2 + p_quadrant[...], 1)
    rows = [group, ez, map_index, apart, to_group, to_ez, kind]
    head = jnp.concatenate(
        [row.astype(f32) for row in rows] + [jnp.zeros((1, capacity), f32)], axis=0
    )
    head_out[...] = head
    here, there = iota((capacity, capacity), 0), iota((capacity, capacity), 1)
    columns = dot_t(one(here == there), head.astype(bf16))
    which_out[...] = columns[:, 2:3]
    source = (columns[:, 0:1] * 16.0 + columns[:, 1:2]).astype(jnp.int32)
    picked_out[...] = one(source == iota((capacity, FACES), 1))
    earlier = (columns[:, 3:4] == apart.astype(f32)) & (here < there)
    position = jnp.sum(jnp.where(earlier, 1.0, 0.0), axis=0, keepdims=True).astype(jnp.int32)
    slot = jnp.where(position < slots, apart * slots + position, -1)
    placed_out[...] = one(iota((ranks * slots, capacity), 0) == slot)

    _, _, fine, coarse = node_tables(NODES)
    lane = iota((8, 128), 1)
    along_a = table_tiles(fine + coarse, lane % 8)
    along_b = table_tiles(fine + coarse, lane // 8 % 8)
    for index in range(CODES):
        first = along_a[index // 4 * 2 + index % 4 // 2]
        second = along_b[index // 4 * 2 + index % 2]
        blocks = []
        for v in range(2):
            kept = jnp.where(lane // 64 == v, first, 0.0)
            blocks += [kept * second[b : b + 1, :] for b in range(8)]
        high, low = split(jnp.concatenate(blocks, axis=0))
        lanes = slice(index * 128, index * 128 + 128)
        maps_high[0:128, lanes] = high
        maps_high[128:256, lanes] = high
        maps_low[:, lanes] = low


def send_kernel(
    ranks, slots, field, count, planned, which_in, picked, placed_in, maps_high, maps_low, *outs
):
    messages, faces_out, x_layers, y_layers = (
        outs[:ranks], outs[ranks], outs[ranks + 1 : ranks + 1 + len(neighbour_messages(ranks))],
        outs[ranks + 1 + len(neighbour_messages(ranks)) :],
    )
    capacity = planned.shape[1]
    lines = iota((8, capacity), 0)
    unused = (lines == 6) & (iota((8, capacity), 1) >= count[...])
    head = jnp.where(unused, 0.0, planned[...]).astype(bf16)
    me = lax.axis_index("elem")
    for i, k in enumerate(neighbour_messages(ranks)):
        for v in range(4):
            x_layers[i][v * 32 : v * 32 + 32, :] = jnp.where(
                me ^ k == me + 1,
                field[v * 256 + 224 : v * 256 + 256, :],
                field[v * 256 : v * 256 + 32, :],
            )
    if len(y_layers) == 1:
        y_layers[0][...] = jnp.where(lax.axis_index("sub") == 0, y_row(field, 31), y_row(field, 0))
    else:
        y_layers[0][...] = y_row(field, 0)
        y_layers[1][...] = y_row(field, 31)

    order = lane_order(False)
    parts = []
    for kind_of in (0, 1):
        blocks = []
        for end in (0, 1):
            for ey in range(EY):
                if kind_of == 0:
                    blocks += [
                        field[pl.ds(v * 256 + (NODES - 1) * end * 32 + ey * 8, 8), :]
                        for v in range(4)
                    ]
                else:
                    blocks.append(y_row(field, ey * 8 + (NODES - 1) * end))
        stacked_high, stacked_low = split(jnp.concatenate(blocks, axis=0))
        moved = dot(jnp.concatenate([stacked_high, stacked_low], axis=1), twice(order))
        turned = block_transpose([moved[g * 32 : (g + 1) * 32] for g in range(8)])
        parts.append(
            jnp.concatenate(
                [turned[b][v * 8 : (v + 1) * 8] for v in range(4) for b in range(8)], axis=0
            )
        )
    ends = jnp.zeros((256, 128), f32)
    for ey in range(EY):
        lines = [y_row(field, ey * 8 + b) for b in range(8)]
        stacked = jnp.concatenate(
            [lines[b][v * 8 : (v + 1) * 8] for v in range(4) for b in range(8)], axis=0
        )
        stacked_high, stacked_low = split(stacked)
        ends += dot(
            jnp.concatenate([stacked_high, stacked_low], axis=1), twice(end_lanes(ey, False))
        )
    parts.append(ends)
    faces = jnp.concatenate(parts, axis=1)
    faces_out[...] = faces

    faces_high, faces_low = split(faces)
    values = dot_t(picked[...], faces_high) + dot_t(picked[...], faces_low)
    which = which_in[...]
    pair = jnp.concatenate([values[:, :128], values[:, 128:]], axis=0)
    pair_high, pair_low = split(pair)
    out = dot(jnp.concatenate([pair_high, pair_low], axis=1), maps_high[...])
    out += dot(pair_high, maps_low[...])
    which = jnp.concatenate([which, which], axis=0)
    for index in range(CODES):
        pair = jnp.where(which == float(index + 1), out[:, index * 128 : (index + 1) * 128], pair)
    mapped = [pair[:capacity], pair[capacity:]]
    mapped_high, mapped_low = split(jnp.concatenate(mapped, axis=1))
    for message, k in zip(messages, send_order(ranks)):
        placed = placed_in[k * slots : (k + 1) * slots, :]
        rows = dot(placed, mapped_high) + dot(placed, mapped_low)
        message[0:slots, :] = rows[:, :128]
        message[slots : 2 * slots, :] = rows[:, 128:]
        message[2 * slots : 2 * slots + 8, :] = jnp.zeros((8, 128), f32)
        message[2 * slots : 2 * slots + 8, 0:slots] = dot_t(head, placed)


def local_kernel(
    ranks, field, register, advect, mixing, drag, after, base, gains
):
    comp = lax.axis_index("comp")
    derivative, scale, _, _ = node_tables(NODES)
    left, right, speed = [], [], []
    for d in range(3):
        a = advect[comp, d]
        speed.append(a)
        left.append(scale * (0.5 * a + 0.5 * upwind_share * jnp.abs(a)))
        right.append(scale * (0.5 * upwind_share * jnp.abs(a) - 0.5 * a))

    me, sub, subs = lax.axis_index("elem"), lax.axis_index("sub"), lax.axis_size("sub")
    values = [drag[comp, v] * scale for v in range(4)]
    values.append(jnp.where(sub > 0, left[1], 0.0))
    values.append(jnp.where(sub < subs - 1, right[1], 0.0))
    for k in neighbour_messages(ranks):
        values.append(jnp.where(me ^ k == me - 1, left[0], 0.0))
        values.append(jnp.where(me ^ k == me + 1, right[0], 0.0))
    line = iota(gains.shape, 0)
    lines = jnp.zeros(gains.shape, f32)
    for i, value in enumerate(values):
        lines = jnp.where(line == i, time_step * value, lines)
    gains[...] = lines
    tile_z, tile_y = table_tiles([derivative, derivative.T], iota((8, 128), 1) % 8)

    def both_ways(row, column, node, gain_left, gain_right):
        first, last = node == 0, node == NODES - 1
        out = jnp.where((row == column) & first, -gain_left, 0.0)
        out = jnp.where((row == column) & last, -gain_right, out)
        out = jnp.where((row == column - 1) & first, gain_left, out)
        return jnp.where((row == column + 1) & last, gain_right, out)

    row, column = iota((128, 128), 0), iota((128, 128), 1)
    along_z = both_ways(row, column, column % 8, left[2], right[2]) - speed[2] * jnp.where(
        row // 8 == column // 8, jnp.concatenate([tile_z] * 16, axis=0), 0.0
    )
    z_high, z_low = split(along_z)
    z_high = twice(z_high)
    row, column = iota((256, 256), 0), iota((256, 256), 1)
    node = row % 8
    tile = jnp.concatenate([tile_y] * 2, axis=1)
    across = jnp.where(
        row // 8 == column // 8, -speed[0] * jnp.concatenate([tile] * 32, axis=0), 0.0
    )
    across += jnp.where((row == column) & (node == 0), -left[0], 0.0)
    across += jnp.where((row == column) & (node == NODES - 1), -right[0], 0.0)
    same = (row // 32 == column // 32) & (node == column % 8)
    mixed = jnp.zeros((256, 256), f32)
    for v in range(4):
        for w in range(4):
            mixed = jnp.where(
                ((row // 8) % 4 == v) & ((column // 8) % 4 == w), mixing[comp, v, w], mixed
            )
    across += jnp.where(same, mixed, 0.0)
    across_high, across_low = split(across)

    for ey in range(EY):
        lines = [y_row(field, ey * 8 + j) for j in range(8)]
        stacked = jnp.concatenate(lines, axis=0)
        stacked_high, stacked_low = split(stacked)
        rate = dot(jnp.concatenate([stacked_high, stacked_low], axis=1), z_high)
        rate += dot(stacked_high, z_low)
        pair = dot(across_high, jnp.concatenate([stacked_high, stacked_low], axis=1))
        rate += pair[:, :128] + pair[:, 128:] + dot(across_low, stacked_high)
        along_y = []
        for m in range(8):
            total = float(derivative[m, 0]) * lines[0]
            for j in range(1, 8):
                total += float(derivative[m, j]) * lines[j]
            total = -speed[1] * total
            if m == 0:
                total -= left[1] * lines[0]
                if ey > 0:
                    total += left[1] * y_row(field, ey * 8 - 1)
            if m == NODES - 1:
                total -= right[1] * lines[m]
                if ey < EY - 1:
                    total += right[1] * y_row(field, ey * 8 + 8)
            along_y.append(total)
        rate += jnp.concatenate(along_y, axis=0)
        kept = jnp.concatenate([y_row(register, ey * 8 + j) for j in range(8)], axis=0)
        base[ey * 256 : (ey + 1) * 256, :] = register_keep * kept + time_step * rate


def finish_kernel(ranks, slots, *refs):
    messages = refs[:ranks]
    base, field, faces, y_before, y_after, gains = refs[ranks : ranks + 6]
    layers = refs[ranks + 6 : -5]
    new_out, advanced_out, new, advanced, left = refs[-5:]
    total = jnp.zeros((FACES, 256), f32)
    masks = jnp.zeros((16, FACES), f32)
    for message in messages:
        head = message[2 * slots : 2 * slots + 8, 0:slots]
        kind = head[6:7]
        target = jnp.where(kind > 0.0, head[4:5] * 16.0 + head[5:6], -1.0).astype(jnp.int32)
        both = jnp.concatenate([target, target], axis=1)
        placed = one(iota((FACES, 2 * slots), 0) == both)
        values = jnp.concatenate([message[0:slots, :], message[slots : 2 * slots, :]], axis=1)
        high = values.astype(bf16).astype(f32)
        total += dot(placed, jnp.concatenate([high, values - high], axis=0).astype(bf16))
        row = iota((16, 2 * slots), 0)
        quadrant = ((row % 8) // 4) * 2 + row // 8
        kind = jnp.where(iota((1, 2 * slots), 1) < slots, jnp.concatenate([kind, kind], axis=1), 0.0)
        live = (kind == 1.0) | (kind == 2.0 + quadrant.astype(f32))
        masks += dot_t(one(live & (kind > 0.0)), placed)
    total = total.T
    terms = []
    for v in range(4):
        gain = gains[v : v + 1, 0:1]
        for b in range(8):
            at = (v * 8 + b) * 8
            count = masks[0:8] if b < 4 else masks[8:16]
            terms.append(gain * (total[at : at + 8] - count * faces[at : at + 8, :]))
    turned = []
    for lanes in (slice(0, 128), slice(128, 256)):
        turned += block_transpose(
            [
                jnp.concatenate([terms[v * 8 + b][:, lanes] for v in range(4)], axis=0)
                for b in range(8)
            ]
        )
    high, low = split(jnp.concatenate(turned, axis=0))
    moved = dot(jnp.concatenate([high, low], axis=1), twice(lane_order(True)))
    high, low = split(jnp.concatenate([term[:, 256:384] for term in terms], axis=0))
    ends = jnp.concatenate([end_lanes(ey, True) for ey in range(EY)], axis=1)
    on_z = dot(jnp.concatenate([high, low], axis=1), twice(ends))

    copies = []
    for v in range(4):
        for ey in range(EY):
            for j in range(8):
                y = ey * 8 + j
                at = (v * 8 + j) * 8
                rate = base[y * 32 + v * 8 : y * 32 + v * 8 + 8, :]
                rate += on_z[at : at + 8, ey * 128 : ey * 128 + 128]
                if j in (0, NODES - 1):
                    at = ((8 + (4 if j else 0) + ey) * 4 + v) * 8
                    rate += moved[at : at + 8]
                if y == 0:
                    rate += gains[4:5, :] * y_before[v * 8 : v * 8 + 8, :]
                if y == 31:
                    rate += gains[5:6, :] * y_after[v * 8 : v * 8 + 8, :]
                new[pl.ds(v * 256 + y, 8, stride=32), :] = rate
        for end in (0, 1):
            at = v * 256 + (NODES - 1) * end * 32
            coupled = jnp.concatenate(
                [
                    moved[((end * 4 + ey) * 4 + v) * 8 : ((end * 4 + ey) * 4 + v) * 8 + 8]
                    for ey in range(EY)
                ],
                axis=0,
            )
            for i in range(len(layers)):
                beside = layers[i][v * 32 : v * 32 + 32, :]
                coupled += gains[6 + 2 * i + end : 7 + 2 * i + end, :] * beside
            new[pl.ds(at, 32), :] = new[pl.ds(at, 32), :] + coupled
        rows = pl.ds(v * 256, 256)
        advanced[rows, :] = field[rows, :] + section_weight * new[rows, :]
        for i, (source, place) in enumerate(((new, new_out), (advanced, advanced_out))):
            copies.append(
                pltpu.make_async_copy(source.at[rows], place.at[rows], left.at[v * 2 + i])
            )
            copies[-1].start()
    for copy in copies:
        copy.wait()


def along(layer, axis, step):
    devices = lax.axis_size(axis)
    pairs = [(i, i + step) for i in range(devices) if 0 <= i + step < devices]
    return lax.ppermute(layer, axis, pairs)


def on_device(
    field, register, advect, mixing, drag, face_elem, face_side, mortar_code, partner_rank,
    partner_elem, partner_side, partner_quadrant, face_count,
):
    ranks = lax.axis_size("elem")
    capacity = face_elem.shape[-1]
    slots = max(2, 2 * capacity // ranks)
    subs = lax.axis_size("sub")
    layers = 1 if subs == 2 else 2
    carriers = neighbour_messages(ranks)
    flat = field.reshape(1024, 128)
    vmem = pl.BlockSpec(memory_space=pltpu.VMEM)
    smem = pl.BlockSpec(memory_space=pltpu.SMEM)
    row = (1, capacity)
    plan = pl.pallas_call(
        functools.partial(plan_kernel, ranks, slots),
        out_shape=[
            jax.ShapeDtypeStruct((8, capacity), f32),
            jax.ShapeDtypeStruct((capacity, 1), f32),
            jax.ShapeDtypeStruct((capacity, FACES), bf16),
            jax.ShapeDtypeStruct((ranks * slots, capacity), bf16),
            jax.ShapeDtypeStruct((256, CODES * 128), bf16),
            jax.ShapeDtypeStruct((128, CODES * 128), bf16),
        ],
        in_specs=[vmem] * 7,
        out_specs=[vmem] * 6,
        compiler_params=pltpu.CompilerParams(vmem_limit_bytes=32 << 20),
        cost_estimate=pl.CostEstimate(flops=10**9, bytes_accessed=8 << 20, transcendentals=0),
        name="plan_records",
    )(
        face_elem.reshape(row), face_side.reshape(row), mortar_code.reshape(row),
        partner_rank.reshape(row), partner_elem.reshape(row), partner_side.reshape(row),
        partner_quadrant.reshape(row),
    )
    face_count, plan = lax.optimization_barrier((face_count, plan))
    outs = pl.pallas_call(
        functools.partial(send_kernel, ranks, slots),
        out_shape=[jax.ShapeDtypeStruct((2 * slots + 8, 128), f32)] * ranks
        + [jax.ShapeDtypeStruct((256, FACES), f32)]
        + [jax.ShapeDtypeStruct((128, 128), f32)] * len(carriers)
        + [jax.ShapeDtypeStruct((32, 128), f32)] * layers,
        in_specs=[vmem] * 8,
        out_specs=[vmem] * (ranks + 1 + len(carriers) + layers),
        compiler_params=pltpu.CompilerParams(vmem_limit_bytes=32 << 20),
        cost_estimate=pl.CostEstimate(flops=10**8, bytes_accessed=2 << 20, transcendentals=0),
        name="send_faces",
    )(flat, face_count.reshape(1, 1), *plan)
    faces, layers_out = outs[ranks], outs[ranks + 1 :]
    outgoing = dict(zip(send_order(ranks), outs))
    received = {}
    for k in send_order(ranks):
        pairs = [(2 * e + c, 2 * (e ^ k) + 1 - c) for e in range(ranks) for c in range(2)]
        received[k] = lax.ppermute(outgoing[k], ("elem", "comp"), pairs)

    layers_out, received[0] = lax.optimization_barrier((layers_out, received[0]))
    x_layers, y_layers = layers_out[: len(carriers)], layers_out[len(carriers) :]
    beside = []
    for k, layer in zip(carriers, x_layers):
        pairs = [(e, e ^ k) for e in range(ranks) if abs((e ^ k) - e) == 1]
        beside.append(lax.ppermute(layer, "elem", pairs))
    if layers == 1:
        y_before = y_after = lax.ppermute(y_layers[0], "sub", [(0, 1), (1, 0)])
    else:
        y_before = along(y_layers[1], "sub", 1)
        y_after = along(y_layers[0], "sub", -1)
    base, gains = pl.pallas_call(
        functools.partial(local_kernel, ranks),
        out_shape=[
            jax.ShapeDtypeStruct((1024, 128), f32),
            jax.ShapeDtypeStruct((16, 128), f32),
        ],
        in_specs=[vmem, vmem, smem, smem, smem, pl.BlockSpec(memory_space=pl.ANY)],
        out_specs=[vmem] * 2,
        compiler_params=pltpu.CompilerParams(vmem_limit_bytes=32 << 20),
        cost_estimate=pl.CostEstimate(flops=5 * 10**8, bytes_accessed=4 << 20, transcendentals=0),
        name="local_rate",
    )(
        flat, register.reshape(1024, 128), advect, mixing, drag, received[0],
    )
    new, advanced = pl.pallas_call(
        functools.partial(finish_kernel, ranks, slots),
        out_shape=[jax.ShapeDtypeStruct((1024, 128), f32)] * 2,
        in_specs=[vmem] * (ranks + 6 + len(carriers)),
        out_specs=[pl.BlockSpec(memory_space=pl.ANY)] * 2,
        scratch_shapes=[pltpu.VMEM((1024, 128), f32)] * 2 + [pltpu.SemaphoreType.DMA((8,))],
        compiler_params=pltpu.CompilerParams(vmem_limit_bytes=32 << 20),
        cost_estimate=pl.CostEstimate(flops=10**8, bytes_accessed=4 << 20, transcendentals=0),
        name="couple_and_finish",
    )(
        *[received[k] for k in send_order(ranks)], base, flat, faces, y_before, y_after, gains, *beside
    )
    return new.reshape(field.shape), advanced.reshape(field.shape)


def solution(mesh):
    block = P("comp", None, ("parts", "elem"), "sub", None)
    records = P("comp", ("parts", "elem"), "sub", None)
    in_specs = (
        block, block, P(), P(), P(), records, records, records,
        P("comp", ("parts", "elem"), "sub", None, None), records, records, records,
        P("comp", ("parts", "elem"), "sub"),
    )
    return jax.shard_map(
        on_device, mesh=mesh, in_specs=in_specs, out_specs=(block, block), check_vma=False
    )
```

```python
import functools
import math

import jax
import jax.numpy as jnp
import numpy as np
from jax import lax
from jax.experimental import pallas as pl
from jax.experimental.pallas import tpu as pltpu
from jax.sharding import PartitionSpec as P

NODES = 8
EY = 4
EZ = 16
FACES = 384
CODES = 8

upwind_share = 0.5
register_keep = -0.4178904745
section_weight = 1.7201463215
time_step = 0.05

f32 = jnp.float32
bf16 = jnp.bfloat16


def legendre_values(point, count):
    values = [1.0, point]
    for power in range(2, count):
        values.append(
            ((2 * power - 1) * point * values[power - 1] - (power - 1) * values[power - 2]) / power
        )
    return values[:count]


def lagrange_rows(points, targets):
    total = len(points)
    result = np.ones((len(targets), total))
    for row, target in enumerate(targets):
        for column in range(total):
            for other in range(total):
                if other != column:
                    result[row, column] *= (target - points[other]) / (
                        points[column] - points[other]
                    )
    return result


@functools.lru_cache
def node_tables(nodes):
    degree = nodes - 1
    guesses = [math.cos(math.pi * position / degree) for position in range(nodes)]
    for sweep in range(100):
        updated = []
        for point in guesses:
            values = legendre_values(point, nodes)
            updated.append(
                point - (point * values[degree] - values[degree - 1]) / (nodes * values[degree])
            )
        guesses = updated
    points = sorted(guesses)
    points[0] = -1.0
    points[-1] = 1.0
    basis = np.array([legendre_values(point, nodes) for point in points])
    inverse = np.linalg.inv(basis)
    barycentric = []
    for position in range(nodes):
        product = 1.0
        for other in range(nodes):
            if other != position:
                product = product * (points[position] - points[other])
        barycentric.append(1.0 / product)
    derivative = np.zeros((nodes, nodes))
    for position in range(nodes):
        for other in range(nodes):
            if other != position:
                derivative[position, other] = (
                    barycentric[other] / barycentric[position] / (points[position] - points[other])
                )
        derivative[position, position] = -derivative[position].sum()
    mask = np.array([[point < 0 for point in points], [point > 0 for point in points]], np.float64)
    fine = [lagrange_rows(points, [(point + shift) / 2.0 for point in points]) for shift in (-1, 1)]
    coarse = []
    for half, shift in ((0, 1.0), (1, -1.0)):
        values = np.array([legendre_values(2.0 * point + shift, nodes) for point in points])
        coarse.append((values * mask[half][:, None]) @ inverse)
    return derivative, degree * nodes / 2.0, fine, coarse


def split(values):
    high = values.astype(bf16)
    return high, (values - high.astype(f32)).astype(bf16)


def dot(left, right):
    return lax.dot_general(left, right, (((1,), (0,)), ((), ())), preferred_element_type=f32)


def dot_t(left, right):
    return lax.dot_general(left, right, (((1,), (1,)), ((), ())), preferred_element_type=f32)


def iota(shape, dim):
    return lax.broadcasted_iota(jnp.int32, shape, dim)


def one(condition):
    return jnp.where(condition, 1.0, 0.0).astype(bf16)


def twice(matrix):
    return jnp.concatenate([matrix, matrix], axis=0)


def block_transpose(parts):
    parts = list(parts)
    block = iota(parts[0].shape, 1) // 16
    for bit in (1, 2, 4):
        upper = (block & bit) != 0
        for g in range(8):
            if g & bit:
                continue
            low, high = parts[g], parts[g | bit]
            parts[g] = jnp.where(upper, pltpu.roll(high, 16 * bit, 1), low)
            parts[g | bit] = jnp.where(upper, high, pltpu.roll(low, 128 - 16 * bit, 1))
    return parts


def lane_order(inverse):
    row, column = iota((128, 128), 1 if inverse else 0), iota((128, 128), 0 if inverse else 1)
    return one(((row // 8) == (column % 16)) & ((row % 8) == (column // 16)))


def end_lanes(ey, inverse):
    z, lane = iota((128, 128), 1 if inverse else 0), iota((128, 128), 0 if inverse else 1)
    return one(
        (lane // 32 == ey) & (z // 8 == lane % 16) & (z % 8 == (NODES - 1) * ((lane // 16) % 2))
    )


def table_tiles(tables, node):
    place = iota((8, 128), 0) * 8 + node
    tiles = [jnp.zeros((8, 128), f32) for _ in tables]
    for i in range(8):
        for j in range(8):
            here = place == i * 8 + j
            tiles = [
                jnp.where(here, float(table[j, i]), tile) for table, tile in zip(tables, tiles)
            ]
    return tiles


def y_row(ref, y):
    return ref[pl.ds(y, 32, stride=32), :]


def face_number(elem, side):
    direction, end = side >> 1, side & 1
    ey, ez = elem >> 4, elem & 15
    group = jnp.where(direction == 2, 16 + 2 * ey + end, direction * 8 + end * 4 + ey)
    return group, ez


def send_order(ranks):
    return list(range(ranks))[::-1]


def neighbour_messages(ranks):
    return [k for k in range(1, ranks) if k & (k + 1) == 0]


def plan_kernel(
    ranks, slots, elem, side, code, rank, p_elem, p_side, p_quadrant,
    head_out, which_out, picked_out, placed_out, maps,
):
    capacity = elem.shape[1]
    me = lax.axis_index("elem")
    group, ez = face_number(elem[...], side[...])
    codes = code[...]
    map_index = jnp.where(codes == 5, 5 + p_quadrant[...], codes)
    apart = rank[...] ^ me
    to_group, to_ez = face_number(p_elem[...], p_side[...])
    kind = jnp.where(codes == 5, 2 + p_quadrant[...], 1)
    rows = [group, ez, map_index, apart, to_group, to_ez, kind]
    head = jnp.concatenate(
        [row.astype(f32) for row in rows] + [jnp.zeros((1, capacity), f32)], axis=0
    )
    head_out[...] = head
    here, there = iota((capacity, capacity), 0), iota((capacity, capacity), 1)
    columns = dot_t(one(here == there), head.astype(bf16))
    which_out[...] = columns[:, 2:3]
    source = (columns[:, 0:1] * 16.0 + columns[:, 1:2]).astype(jnp.int32)
    picked_out[...] = one(source == iota((capacity, FACES), 1))
    earlier = (columns[:, 3:4] == apart.astype(f32)) & (here < there)
    position = jnp.sum(jnp.where(earlier, 1.0, 0.0), axis=0, keepdims=True).astype(jnp.int32)
    slot = jnp.where(position < slots, apart * slots + position, -1)
    placed_out[...] = one(iota((ranks * slots, capacity), 0) == slot)

    _, _, fine, coarse = node_tables(NODES)
    lane = iota((8, 128), 1)
    along_a = table_tiles(fine + coarse, lane % 8)
    along_b = table_tiles(fine + coarse, lane // 8 % 8)
    lower = lane < 64
    for pair in range(CODES // 2):
        tiles = []
        for index in (2 * pair, 2 * pair + 1):
            tiles.append(
                (along_a[index // 4 * 2 + index % 4 // 2], along_b[index // 4 * 2 + index % 2])
            )
        first = jnp.where(lower, tiles[0][0], tiles[1][0])
        second = jnp.where(lower, tiles[0][1], tiles[1][1])
        high, low = split(
            jnp.concatenate([first * second[b : b + 1, :] for b in range(8)], axis=0)
        )
        lanes = slice(pair * 128, pair * 128 + 128)
        maps[0:64, lanes] = high
        maps[64:128, lanes] = high
        maps[128:192, lanes] = low
        maps[192:256, lanes] = jnp.zeros((64, 128), bf16)


def send_kernel(
    ranks, slots, field, count, planned, which_in, picked, placed_in, maps, *outs
):
    messages, faces_out = outs[:ranks], outs[ranks]
    capacity = planned.shape[1]
    lines = iota((8, capacity), 0)
    unused = (lines == 6) & (iota((8, capacity), 1) >= count[...])
    head = jnp.where(unused, 0.0, planned[...]).astype(bf16)
    order = lane_order(False)
    parts = []
    for kind_of in (0, 1):
        blocks = []
        for end in (0, 1):
            for ey in range(EY):
                if kind_of == 0:
                    blocks += [
                        field[pl.ds(v * 256 + (NODES - 1) * end * 32 + ey * 8, 8), :]
                        for v in range(4)
                    ]
                else:
                    blocks.append(y_row(field, ey * 8 + (NODES - 1) * end))
        stacked_high, stacked_low = split(jnp.concatenate(blocks, axis=0))
        moved = dot(jnp.concatenate([stacked_high, stacked_low], axis=1), twice(order))
        turned = block_transpose([moved[g * 32 : (g + 1) * 32] for g in range(8)])
        parts.append(
            jnp.concatenate(
                [turned[b][v * 8 : (v + 1) * 8] for v in range(4) for b in range(8)], axis=0
            )
        )
    ends = jnp.zeros((256, 128), f32)
    for ey in range(EY):
        lines = [y_row(field, ey * 8 + b) for b in range(8)]
        stacked = jnp.concatenate(
            [lines[b][v * 8 : (v + 1) * 8] for v in range(4) for b in range(8)], axis=0
        )
        stacked_high, stacked_low = split(stacked)
        ends += dot(
            jnp.concatenate([stacked_high, stacked_low], axis=1), twice(end_lanes(ey, False))
        )
    parts.append(ends)
    faces = jnp.concatenate(parts, axis=1)
    faces_out[...] = faces

    faces_high, faces_low = split(faces)
    values = dot_t(
        jnp.concatenate([picked[...], picked[...]], axis=1),
        jnp.concatenate([faces_high, faces_low], axis=1),
    )
    lower = iota((capacity, 128), 1) < 64
    halves = [values[:, :128], values[:, 128:]]
    stacked = []
    for half in halves:
        crossed = pltpu.roll(half, 64, 1)
        high, crossed_high = [part.astype(bf16).astype(f32) for part in (half, crossed)]
        low, crossed_low = half - high, crossed - crossed_high
        stacked.append(jnp.concatenate([jnp.where(lower, high, crossed_low), high], axis=1))
        stacked.append(
            jnp.concatenate([jnp.where(lower, crossed_high, low), crossed_high], axis=1)
        )
    out = dot(jnp.concatenate(stacked, axis=0).astype(bf16), maps[...])
    which = which_in[...].astype(jnp.int32)
    column, odd = (which - 1) >> 1, (which - 1) & 1
    mapped = []
    for h, half in enumerate(halves):
        sides = []
        for v in (2 * h, 2 * h + 1):
            rows = out[v * capacity : (v + 1) * capacity]
            taken = rows[:, :128]
            for pair in range(1, CODES // 2):
                taken = jnp.where(column == pair, rows[:, pair * 128 : pair * 128 + 128], taken)
            sides.append(jnp.where(odd == v % 2, taken, pltpu.roll(taken, 64, 1)))
        mapped.append(jnp.where(which == 0, half, jnp.where(lower, sides[0], sides[1])))
    mapped_high, mapped_low = split(jnp.concatenate(mapped, axis=1))
    rows = dot(placed_in[...], mapped_high) + dot(placed_in[...], mapped_low)
    heads = dot_t(head, placed_in[...])
    for message, k in zip(messages, send_order(ranks)):
        here = slice(k * slots, (k + 1) * slots)
        message[0:slots, :] = rows[here, :128]
        message[slots : 2 * slots, :] = rows[here, 128:]
        message[2 * slots : 2 * slots + 8, :] = jnp.zeros((8, 128), f32)
        message[2 * slots : 2 * slots + 8, 0:slots] = heads[:, here]


def layers_kernel(ranks, field, after, *outs):
    carriers = len(neighbour_messages(ranks))
    x_layers, y_layers = outs[:carriers], outs[carriers:]
    me = lax.axis_index("elem")
    for i, k in enumerate(neighbour_messages(ranks)):
        for v in range(4):
            x_layers[i][v * 32 : v * 32 + 32, :] = jnp.where(
                me ^ k == me + 1,
                field[v * 256 + 224 : v * 256 + 256, :],
                field[v * 256 : v * 256 + 32, :],
            )
    if len(y_layers) == 1:
        y_layers[0][...] = jnp.where(lax.axis_index("sub") == 0, y_row(field, 31), y_row(field, 0))
    else:
        y_layers[0][...] = y_row(field, 0)
        y_layers[1][...] = y_row(field, 31)


def local_kernel(
    ranks, field, register, advect, mixing, drag, after, base, gains
):
    comp = lax.axis_index("comp")
    derivative, scale, _, _ = node_tables(NODES)
    left, right, speed = [], [], []
    for d in range(3):
        a = advect[comp, d]
        speed.append(a)
        left.append(scale * (0.5 * a + 0.5 * upwind_share * jnp.abs(a)))
        right.append(scale * (0.5 * upwind_share * jnp.abs(a) - 0.5 * a))

    me, sub, subs = lax.axis_index("elem"), lax.axis_index("sub"), lax.axis_size("sub")
    values = [drag[comp, v] * scale for v in range(4)]
    values.append(jnp.where(sub > 0, left[1], 0.0))
    values.append(jnp.where(sub < subs - 1, right[1], 0.0))
    for k in neighbour_messages(ranks):
        values.append(jnp.where(me ^ k == me - 1, left[0], 0.0))
        values.append(jnp.where(me ^ k == me + 1, right[0], 0.0))
    line = iota(gains.shape, 0)
    lines = jnp.zeros(gains.shape, f32)
    for i, value in enumerate(values):
        lines = jnp.where(line == i, time_step * value, lines)
    gains[...] = lines
    tile_z, tile_y = table_tiles([derivative, derivative.T], iota((8, 128), 1) % 8)

    def both_ways(row, column, node, gain_left, gain_right):
        first, last = node == 0, node == NODES - 1
        out = jnp.where((row == column) & first, -gain_left, 0.0)
        out = jnp.where((row == column) & last, -gain_right, out)
        out = jnp.where((row == column - 1) & first, gain_left, out)
        return jnp.where((row == column + 1) & last, gain_right, out)

    row, column = iota((128, 128), 0), iota((128, 128), 1)
    along_z = both_ways(row, column, column % 8, left[2], right[2]) - speed[2] * jnp.where(
        row // 8 == column // 8, jnp.concatenate([tile_z] * 16, axis=0), 0.0
    )
    z_high, z_low = split(along_z)
    z_high = twice(z_high)
    row, column = iota((256, 256), 0), iota((256, 256), 1)
    node = row % 8
    tile = jnp.concatenate([tile_y] * 2, axis=1)
    across = jnp.where(
        row // 8 == column // 8, -speed[0] * jnp.concatenate([tile] * 32, axis=0), 0.0
    )
    across += jnp.where((row == column) & (node == 0), -left[0], 0.0)
    across += jnp.where((row == column) & (node == NODES - 1), -right[0], 0.0)
    same = (row // 32 == column // 32) & (node == column % 8)
    mixed = jnp.zeros((256, 256), f32)
    for v in range(4):
        for w in range(4):
            mixed = jnp.where(
                ((row // 8) % 4 == v) & ((column // 8) % 4 == w), mixing[comp, v, w], mixed
            )
    across += jnp.where(same, mixed, 0.0)
    across_high, across_low = split(across)

    for ey in range(EY):
        lines = [y_row(field, ey * 8 + j) for j in range(8)]
        stacked = jnp.concatenate(lines, axis=0)
        stacked_high, stacked_low = split(stacked)
        rate = dot(jnp.concatenate([stacked_high, stacked_low], axis=1), z_high)
        rate += dot(stacked_high, z_low)
        pair = dot(across_high, jnp.concatenate([stacked_high, stacked_low], axis=1))
        rate += pair[:, :128] + pair[:, 128:] + dot(across_low, stacked_high)
        along_y = []
        for m in range(8):
            total = float(derivative[m, 0]) * lines[0]
            for j in range(1, 8):
                total += float(derivative[m, j]) * lines[j]
            total = -speed[1] * total
            if m == 0:
                total -= left[1] * lines[0]
                if ey > 0:
                    total += left[1] * y_row(field, ey * 8 - 1)
            if m == NODES - 1:
                total -= right[1] * lines[m]
                if ey < EY - 1:
                    total += right[1] * y_row(field, ey * 8 + 8)
            along_y.append(total)
        rate += jnp.concatenate(along_y, axis=0)
        kept = jnp.concatenate([y_row(register, ey * 8 + j) for j in range(8)], axis=0)
        base[ey * 256 : (ey + 1) * 256, :] = register_keep * kept + time_step * rate


def finish_kernel(ranks, slots, *refs):
    messages = refs[:ranks]
    base, field, faces, y_before, y_after, gains = refs[ranks : ranks + 6]
    layers = refs[ranks + 6 : -5]
    new_out, advanced_out, new, advanced, left = refs[-5:]
    total = jnp.zeros((FACES, 256), f32)
    masks = jnp.zeros((16, FACES), f32)
    for message in messages:
        head = message[2 * slots : 2 * slots + 8, 0:slots]
        kind = head[6:7]
        target = jnp.where(kind > 0.0, head[4:5] * 16.0 + head[5:6], -1.0).astype(jnp.int32)
        both = jnp.concatenate([target, target], axis=1)
        placed = one(iota((FACES, 2 * slots), 0) == both)
        values = jnp.concatenate([message[0:slots, :], message[slots : 2 * slots, :]], axis=1)
        high = values.astype(bf16).astype(f32)
        total += dot(placed, jnp.concatenate([high, values - high], axis=0).astype(bf16))
        row = iota((16, 2 * slots), 0)
        quadrant = ((row % 8) // 4) * 2 + row // 8
        kind = jnp.where(iota((1, 2 * slots), 1) < slots, jnp.concatenate([kind, kind], axis=1), 0.0)
        live = (kind == 1.0) | (kind == 2.0 + quadrant.astype(f32))
        masks += dot_t(one(live & (kind > 0.0)), placed)
    total = total.T
    terms = []
    for v in range(4):
        gain = gains[v : v + 1, 0:1]
        for b in range(8):
            at = (v * 8 + b) * 8
            count = masks[0:8] if b < 4 else masks[8:16]
            terms.append(gain * (total[at : at + 8] - count * faces[at : at + 8, :]))
    turned = []
    for lanes in (slice(0, 128), slice(128, 256)):
        turned += block_transpose(
            [
                jnp.concatenate([terms[v * 8 + b][:, lanes] for v in range(4)], axis=0)
                for b in range(8)
            ]
        )
    high, low = split(jnp.concatenate(turned, axis=0))
    moved = dot(jnp.concatenate([high, low], axis=1), twice(lane_order(True)))
    high, low = split(jnp.concatenate([term[:, 256:384] for term in terms], axis=0))
    ends = jnp.concatenate([end_lanes(ey, True) for ey in range(EY)], axis=1)
    on_z = dot(jnp.concatenate([high, low], axis=1), twice(ends))

    copies = []
    for v in range(4):
        for ey in range(EY):
            for j in range(8):
                y = ey * 8 + j
                at = (v * 8 + j) * 8
                rate = base[y * 32 + v * 8 : y * 32 + v * 8 + 8, :]
                rate += on_z[at : at + 8, ey * 128 : ey * 128 + 128]
                if j in (0, NODES - 1):
                    at = ((8 + (4 if j else 0) + ey) * 4 + v) * 8
                    rate += moved[at : at + 8]
                if y == 0:
                    rate += gains[4:5, :] * y_before[v * 8 : v * 8 + 8, :]
                if y == 31:
                    rate += gains[5:6, :] * y_after[v * 8 : v * 8 + 8, :]
                new[pl.ds(v * 256 + y, 8, stride=32), :] = rate
        for end in (0, 1):
            at = v * 256 + (NODES - 1) * end * 32
            coupled = jnp.concatenate(
                [
                    moved[((end * 4 + ey) * 4 + v) * 8 : ((end * 4 + ey) * 4 + v) * 8 + 8]
                    for ey in range(EY)
                ],
                axis=0,
            )
            for i in range(len(layers)):
                beside = layers[i][v * 32 : v * 32 + 32, :]
                coupled += gains[6 + 2 * i + end : 7 + 2 * i + end, :] * beside
            new[pl.ds(at, 32), :] = new[pl.ds(at, 32), :] + coupled
        rows = pl.ds(v * 256, 256)
        advanced[rows, :] = field[rows, :] + section_weight * new[rows, :]
        for i, (source, place) in enumerate(((new, new_out), (advanced, advanced_out))):
            copies.append(
                pltpu.make_async_copy(source.at[rows], place.at[rows], left.at[v * 2 + i])
            )
            copies[-1].start()
    for copy in copies:
        copy.wait()


def along(layer, axis, step):
    devices = lax.axis_size(axis)
    pairs = [(i, i + step) for i in range(devices) if 0 <= i + step < devices]
    return lax.ppermute(layer, axis, pairs)


def on_device(
    field, register, advect, mixing, drag, face_elem, face_side, mortar_code, partner_rank,
    partner_elem, partner_side, partner_quadrant, face_count,
):
    ranks = lax.axis_size("elem")
    capacity = face_elem.shape[-1]
    slots = max(2, 2 * capacity // ranks)
    subs = lax.axis_size("sub")
    layers = 1 if subs == 2 else 2
    carriers = neighbour_messages(ranks)
    flat = field.reshape(1024, 128)
    vmem = pl.BlockSpec(memory_space=pltpu.VMEM)
    smem = pl.BlockSpec(memory_space=pltpu.SMEM)
    row = (1, capacity)
    plan = pl.pallas_call(
        functools.partial(plan_kernel, ranks, slots),
        out_shape=[
            jax.ShapeDtypeStruct((8, capacity), f32),
            jax.ShapeDtypeStruct((capacity, 1), f32),
            jax.ShapeDtypeStruct((capacity, FACES), bf16),
            jax.ShapeDtypeStruct((ranks * slots, capacity), bf16),
            jax.ShapeDtypeStruct((256, CODES * 64), bf16),
        ],
        in_specs=[vmem] * 7,
        out_specs=[vmem] * 5,
        compiler_params=pltpu.CompilerParams(vmem_limit_bytes=32 << 20),
        cost_estimate=pl.CostEstimate(flops=10**9, bytes_accessed=8 << 20, transcendentals=0),
        name="plan_records",
    )(
        face_elem.reshape(row), face_side.reshape(row), mortar_code.reshape(row),
        partner_rank.reshape(row), partner_elem.reshape(row), partner_side.reshape(row),
        partner_quadrant.reshape(row),
    )
    face_count, plan = lax.optimization_barrier((face_count, plan))
    outs = pl.pallas_call(
        functools.partial(send_kernel, ranks, slots),
        out_shape=[jax.ShapeDtypeStruct((2 * slots + 8, 128), f32)] * ranks
        + [jax.ShapeDtypeStruct((256, FACES), f32)],
        in_specs=[vmem] * 7,
        out_specs=[vmem] * (ranks + 1),
        compiler_params=pltpu.CompilerParams(vmem_limit_bytes=32 << 20),
        cost_estimate=pl.CostEstimate(flops=10**8, bytes_accessed=2 << 20, transcendentals=0),
        name="send_faces",
    )(flat, face_count.reshape(1, 1), *plan)
    faces = outs[ranks]
    outgoing = dict(zip(send_order(ranks), outs))
    received = {}
    for k in send_order(ranks):
        pairs = [(2 * e + c, 2 * (e ^ k) + 1 - c) for e in range(ranks) for c in range(2)]
        received[k] = lax.ppermute(outgoing[k], ("elem", "comp"), pairs)

    layers_out = pl.pallas_call(
        functools.partial(layers_kernel, ranks),
        out_shape=[jax.ShapeDtypeStruct((128, 128), f32)] * len(carriers)
        + [jax.ShapeDtypeStruct((32, 128), f32)] * layers,
        in_specs=[vmem, pl.BlockSpec(memory_space=pl.ANY)],
        out_specs=[vmem] * (len(carriers) + layers),
        compiler_params=pltpu.CompilerParams(vmem_limit_bytes=8 << 20),
        cost_estimate=pl.CostEstimate(flops=10**4, bytes_accessed=1 << 18, transcendentals=0),
        name="halo_layers",
    )(flat, received[0])
    x_layers, y_layers = layers_out[: len(carriers)], layers_out[len(carriers) :]
    beside = []
    for k, layer in zip(carriers, x_layers):
        pairs = [(e, e ^ k) for e in range(ranks) if abs((e ^ k) - e) == 1]
        beside.append(lax.ppermute(layer, "elem", pairs))
    if layers == 1:
        y_before = y_after = lax.ppermute(y_layers[0], "sub", [(0, 1), (1, 0)])
    else:
        y_before = along(y_layers[1], "sub", 1)
        y_after = along(y_layers[0], "sub", -1)
    base, gains = pl.pallas_call(
        functools.partial(local_kernel, ranks),
        out_shape=[
            jax.ShapeDtypeStruct((1024, 128), f32),
            jax.ShapeDtypeStruct((16, 128), f32),
        ],
        in_specs=[vmem, vmem, smem, smem, smem, pl.BlockSpec(memory_space=pl.ANY)],
        out_specs=[vmem] * 2,
        compiler_params=pltpu.CompilerParams(vmem_limit_bytes=32 << 20),
        cost_estimate=pl.CostEstimate(flops=5 * 10**8, bytes_accessed=4 << 20, transcendentals=0),
        name="local_rate",
    )(
        flat, register.reshape(1024, 128), advect, mixing, drag, received[0],
    )
    new, advanced = pl.pallas_call(
        functools.partial(finish_kernel, ranks, slots),
        out_shape=[jax.ShapeDtypeStruct((1024, 128), f32)] * 2,
        in_specs=[vmem] * (ranks + 6 + len(carriers)),
        out_specs=[pl.BlockSpec(memory_space=pl.ANY)] * 2,
        scratch_shapes=[pltpu.VMEM((1024, 128), f32)] * 2 + [pltpu.SemaphoreType.DMA((8,))],
        compiler_params=pltpu.CompilerParams(vmem_limit_bytes=32 << 20),
        cost_estimate=pl.CostEstimate(flops=10**8, bytes_accessed=4 << 20, transcendentals=0),
        name="couple_and_finish",
    )(
        *[received[k] for k in send_order(ranks)], base, flat, faces, y_before, y_after, gains, *beside
    )
    return new.reshape(field.shape), advanced.reshape(field.shape)


def solution(mesh):
    block = P("comp", None, ("parts", "elem"), "sub", None)
    records = P("comp", ("parts", "elem"), "sub", None)
    in_specs = (
        block, block, P(), P(), P(), records, records, records,
        P("comp", ("parts", "elem"), "sub", None, None), records, records, records,
        P("comp", ("parts", "elem"), "sub"),
    )
    return jax.shard_map(
        on_device, mesh=mesh, in_specs=in_specs, out_specs=(block, block), check_vma=False
    )
```

```python
import functools
import math

import jax
import jax.numpy as jnp
import numpy as np
from jax import lax
from jax.experimental import pallas as pl
from jax.experimental.pallas import tpu as pltpu
from jax.sharding import PartitionSpec as P

NODES = 8
EY = 4
EZ = 16
FACES = 384
CODES = 8

upwind_share = 0.5
register_keep = -0.4178904745
section_weight = 1.7201463215
time_step = 0.05

f32 = jnp.float32
bf16 = jnp.bfloat16


def legendre_values(point, count):
    values = [1.0, point]
    for power in range(2, count):
        values.append(
            ((2 * power - 1) * point * values[power - 1] - (power - 1) * values[power - 2]) / power
        )
    return values[:count]


def lagrange_rows(points, targets):
    total = len(points)
    result = np.ones((len(targets), total))
    for row, target in enumerate(targets):
        for column in range(total):
            for other in range(total):
                if other != column:
                    result[row, column] *= (target - points[other]) / (
                        points[column] - points[other]
                    )
    return result


@functools.lru_cache
def node_tables(nodes):
    degree = nodes - 1
    guesses = [math.cos(math.pi * position / degree) for position in range(nodes)]
    for sweep in range(100):
        updated = []
        for point in guesses:
            values = legendre_values(point, nodes)
            updated.append(
                point - (point * values[degree] - values[degree - 1]) / (nodes * values[degree])
            )
        guesses = updated
    points = sorted(guesses)
    points[0] = -1.0
    points[-1] = 1.0
    basis = np.array([legendre_values(point, nodes) for point in points])
    inverse = np.linalg.inv(basis)
    barycentric = []
    for position in range(nodes):
        product = 1.0
        for other in range(nodes):
            if other != position:
                product = product * (points[position] - points[other])
        barycentric.append(1.0 / product)
    derivative = np.zeros((nodes, nodes))
    for position in range(nodes):
        for other in range(nodes):
            if other != position:
                derivative[position, other] = (
                    barycentric[other] / barycentric[position] / (points[position] - points[other])
                )
        derivative[position, position] = -derivative[position].sum()
    mask = np.array([[point < 0 for point in points], [point > 0 for point in points]], np.float64)
    fine = [lagrange_rows(points, [(point + shift) / 2.0 for point in points]) for shift in (-1, 1)]
    coarse = []
    for half, shift in ((0, 1.0), (1, -1.0)):
        values = np.array([legendre_values(2.0 * point + shift, nodes) for point in points])
        coarse.append((values * mask[half][:, None]) @ inverse)
    return derivative, degree * nodes / 2.0, fine, coarse


def split(values):
    high = values.astype(bf16)
    return high, (values - high.astype(f32)).astype(bf16)


def dot(left, right):
    return lax.dot_general(left, right, (((1,), (0,)), ((), ())), preferred_element_type=f32)


def dot_t(left, right):
    return lax.dot_general(left, right, (((1,), (1,)), ((), ())), preferred_element_type=f32)


def iota(shape, dim):
    return lax.broadcasted_iota(jnp.int32, shape, dim)


def one(condition):
    return jnp.where(condition, 1.0, 0.0).astype(bf16)


def twice(matrix):
    return jnp.concatenate([matrix, matrix], axis=0)


def block_transpose(parts):
    parts = list(parts)
    block = iota(parts[0].shape, 1) // 16
    for bit in (1, 2, 4):
        upper = (block & bit) != 0
        for g in range(8):
            if g & bit:
                continue
            low, high = parts[g], parts[g | bit]
            parts[g] = jnp.where(upper, pltpu.roll(high, 16 * bit, 1), low)
            parts[g | bit] = jnp.where(upper, high, pltpu.roll(low, 128 - 16 * bit, 1))
    return parts


def lane_order(inverse):
    row, column = iota((128, 128), 1 if inverse else 0), iota((128, 128), 0 if inverse else 1)
    return one(((row // 8) == (column % 16)) & ((row % 8) == (column // 16)))


def end_lanes(ey, inverse):
    z, lane = iota((128, 128), 1 if inverse else 0), iota((128, 128), 0 if inverse else 1)
    return one(
        (lane // 32 == ey) & (z // 8 == lane % 16) & (z % 8 == (NODES - 1) * ((lane // 16) % 2))
    )


def table_tiles(tables, node):
    place = iota((8, 128), 0) * 8 + node
    tiles = [jnp.zeros((8, 128), f32) for _ in tables]
    for i in range(8):
        for j in range(8):
            here = place == i * 8 + j
            tiles = [
                jnp.where(here, float(table[j, i]), tile) for table, tile in zip(tables, tiles)
            ]
    return tiles


def y_row(ref, y):
    return ref[pl.ds(y, 32, stride=32), :]


def face_number(elem, side):
    direction, end = side >> 1, side & 1
    ey, ez = elem >> 4, elem & 15
    group = jnp.where(direction == 2, 16 + 2 * ey + end, direction * 8 + end * 4 + ey)
    return group, ez


def send_order(ranks):
    near = neighbour_messages(ranks)[::-1]
    return near + [k for k in range(1, ranks)[::-1] if k not in near] + [0]


def neighbour_messages(ranks):
    return [k for k in range(1, ranks) if k & (k + 1) == 0]


def plan_kernel(
    ranks, slots, elem, side, code, rank, p_elem, p_side, p_quadrant,
    head_out, which_out, picked_out, placed_out, maps,
):
    capacity = elem.shape[1]
    me = lax.axis_index("elem")
    group, ez = face_number(elem[...], side[...])
    codes = code[...]
    map_index = jnp.where(codes == 5, 5 + p_quadrant[...], codes)
    apart = rank[...] ^ me
    to_group, to_ez = face_number(p_elem[...], p_side[...])
    kind = jnp.where(codes == 5, 2 + p_quadrant[...], 1)
    rows = [group, ez, map_index, apart, to_group, to_ez, kind]
    head = jnp.concatenate(
        [row.astype(f32) for row in rows] + [jnp.zeros((1, capacity), f32)], axis=0
    )
    head_out[...] = head
    here, there = iota((capacity, capacity), 0), iota((capacity, capacity), 1)
    columns = dot_t(one(here == there), head.astype(bf16))
    which_out[...] = columns[:, 2:3]
    source = (columns[:, 0:1] * 16.0 + columns[:, 1:2]).astype(jnp.int32)
    picked_out[...] = one(source == iota((capacity, FACES), 1))
    earlier = (columns[:, 3:4] == apart.astype(f32)) & (here < there)
    position = jnp.sum(jnp.where(earlier, 1.0, 0.0), axis=0, keepdims=True).astype(jnp.int32)
    slot = jnp.where(position < slots, apart * slots + position, -1)
    placed_out[...] = one(iota((ranks * slots, capacity), 0) == slot)

    _, _, fine, coarse = node_tables(NODES)
    lane = iota((8, 128), 1)
    along_a = table_tiles(fine + coarse, lane % 8)
    along_b = table_tiles(fine + coarse, lane // 8 % 8)
    lower = lane < 64
    for pair in range(CODES // 2):
        tiles = []
        for index in (2 * pair, 2 * pair + 1):
            tiles.append(
                (along_a[index // 4 * 2 + index % 4 // 2], along_b[index // 4 * 2 + index % 2])
            )
        first = jnp.where(lower, tiles[0][0], tiles[1][0])
        second = jnp.where(lower, tiles[0][1], tiles[1][1])
        high, low = split(
            jnp.concatenate([first * second[b : b + 1, :] for b in range(8)], axis=0)
        )
        lanes = slice(pair * 128, pair * 128 + 128)
        maps[0:64, lanes] = high
        maps[64:128, lanes] = high
        maps[128:192, lanes] = low
        maps[192:256, lanes] = jnp.zeros((64, 128), bf16)


def send_kernel(
    ranks, slots, field, count, planned, which_in, picked, placed_in, maps, *outs
):
    messages, faces_out = outs[:ranks], outs[ranks]
    capacity = planned.shape[1]
    lines = iota((8, capacity), 0)
    unused = (lines == 6) & (iota((8, capacity), 1) >= count[...])
    head = jnp.where(unused, 0.0, planned[...]).astype(bf16)
    order = lane_order(False)
    parts = []
    for kind_of in (0, 1):
        blocks = []
        for end in (0, 1):
            for ey in range(EY):
                if kind_of == 0:
                    blocks += [
                        field[pl.ds(v * 256 + (NODES - 1) * end * 32 + ey * 8, 8), :]
                        for v in range(4)
                    ]
                else:
                    blocks.append(y_row(field, ey * 8 + (NODES - 1) * end))
        stacked_high, stacked_low = split(jnp.concatenate(blocks, axis=0))
        moved = dot(jnp.concatenate([stacked_high, stacked_low], axis=1), twice(order))
        turned = block_transpose([moved[g * 32 : (g + 1) * 32] for g in range(8)])
        parts.append(
            jnp.concatenate(
                [turned[b][v * 8 : (v + 1) * 8] for v in range(4) for b in range(8)], axis=0
            )
        )
    ends = jnp.zeros((256, 128), f32)
    for ey in range(EY):
        lines = [y_row(field, ey * 8 + b) for b in range(8)]
        stacked = jnp.concatenate(
            [lines[b][v * 8 : (v + 1) * 8] for v in range(4) for b in range(8)], axis=0
        )
        stacked_high, stacked_low = split(stacked)
        ends += dot(
            jnp.concatenate([stacked_high, stacked_low], axis=1), twice(end_lanes(ey, False))
        )
    parts.append(ends)
    faces = jnp.concatenate(parts, axis=1)
    faces_out[...] = faces

    faces_high, faces_low = split(faces)
    values = dot_t(
        jnp.concatenate([picked[...], picked[...]], axis=1),
        jnp.concatenate([faces_high, faces_low], axis=1),
    )
    lower = iota((capacity, 128), 1) < 64
    halves = [values[:, :128], values[:, 128:]]
    stacked = []
    for half in halves:
        crossed = pltpu.roll(half, 64, 1)
        high, crossed_high = [part.astype(bf16).astype(f32) for part in (half, crossed)]
        low, crossed_low = half - high, crossed - crossed_high
        stacked.append(jnp.concatenate([jnp.where(lower, high, crossed_low), high], axis=1))
        stacked.append(
            jnp.concatenate([jnp.where(lower, crossed_high, low), crossed_high], axis=1)
        )
    out = dot(jnp.concatenate(stacked, axis=0).astype(bf16), maps[...])
    which = which_in[...].astype(jnp.int32)
    column, odd = (which - 1) >> 1, (which - 1) & 1
    mapped = []
    for h, half in enumerate(halves):
        sides = []
        for v in (2 * h, 2 * h + 1):
            rows = out[v * capacity : (v + 1) * capacity]
            taken = rows[:, :128]
            for pair in range(1, CODES // 2):
                taken = jnp.where(column == pair, rows[:, pair * 128 : pair * 128 + 128], taken)
            sides.append(jnp.where(odd == v % 2, taken, pltpu.roll(taken, 64, 1)))
        mapped.append(jnp.where(which == 0, half, jnp.where(lower, sides[0], sides[1])))
    mapped_high, mapped_low = split(jnp.concatenate(mapped, axis=1))
    rows = dot(placed_in[...], mapped_high) + dot(placed_in[...], mapped_low)
    heads = dot_t(head, placed_in[...])
    for message, k in zip(messages, send_order(ranks)):
        here = slice(k * slots, (k + 1) * slots)
        message[0:slots, :] = rows[here, :128]
        message[slots : 2 * slots, :] = rows[here, 128:]
        message[2 * slots : 2 * slots + 8, :] = jnp.zeros((8, 128), f32)
        message[2 * slots : 2 * slots + 8, 0:slots] = heads[:, here]


def layers_kernel(ranks, field, after, *outs):
    carriers = len(neighbour_messages(ranks))
    x_layers, y_layers = outs[:carriers], outs[carriers:]
    me = lax.axis_index("elem")
    for i, k in enumerate(neighbour_messages(ranks)):
        for v in range(4):
            x_layers[i][v * 32 : v * 32 + 32, :] = jnp.where(
                me ^ k == me + 1,
                field[v * 256 + 224 : v * 256 + 256, :],
                field[v * 256 : v * 256 + 32, :],
            )
    if len(y_layers) == 1:
        y_layers[0][...] = jnp.where(lax.axis_index("sub") == 0, y_row(field, 31), y_row(field, 0))
    else:
        y_layers[0][...] = y_row(field, 0)
        y_layers[1][...] = y_row(field, 31)


def local_kernel(
    ranks, field, register, advect, mixing, drag, after, base, gains
):
    comp = lax.axis_index("comp")
    derivative, scale, _, _ = node_tables(NODES)
    left, right, speed = [], [], []
    for d in range(3):
        a = advect[comp, d]
        speed.append(a)
        left.append(scale * (0.5 * a + 0.5 * upwind_share * jnp.abs(a)))
        right.append(scale * (0.5 * upwind_share * jnp.abs(a) - 0.5 * a))

    me, sub, subs = lax.axis_index("elem"), lax.axis_index("sub"), lax.axis_size("sub")
    values = [drag[comp, v] * scale for v in range(4)]
    values.append(jnp.where(sub > 0, left[1], 0.0))
    values.append(jnp.where(sub < subs - 1, right[1], 0.0))
    for k in neighbour_messages(ranks):
        values.append(jnp.where(me ^ k == me - 1, left[0], 0.0))
        values.append(jnp.where(me ^ k == me + 1, right[0], 0.0))
    line = iota(gains.shape, 0)
    lines = jnp.zeros(gains.shape, f32)
    for i, value in enumerate(values):
        lines = jnp.where(line == i, time_step * value, lines)
    gains[...] = lines
    tile_z, tile_y = table_tiles([derivative, derivative.T], iota((8, 128), 1) % 8)

    def both_ways(row, column, node, gain_left, gain_right):
        first, last = node == 0, node == NODES - 1
        out = jnp.where((row == column) & first, -gain_left, 0.0)
        out = jnp.where((row == column) & last, -gain_right, out)
        out = jnp.where((row == column - 1) & first, gain_left, out)
        return jnp.where((row == column + 1) & last, gain_right, out)

    row, column = iota((128, 128), 0), iota((128, 128), 1)
    along_z = both_ways(row, column, column % 8, left[2], right[2]) - speed[2] * jnp.where(
        row // 8 == column // 8, jnp.concatenate([tile_z] * 16, axis=0), 0.0
    )
    z_high, z_low = split(along_z)
    z_high = twice(z_high)
    row, column = iota((256, 256), 0), iota((256, 256), 1)
    node = row % 8
    tile = jnp.concatenate([tile_y] * 2, axis=1)
    across = jnp.where(
        row // 8 == column // 8, -speed[0] * jnp.concatenate([tile] * 32, axis=0), 0.0
    )
    across += jnp.where((row == column) & (node == 0), -left[0], 0.0)
    across += jnp.where((row == column) & (node == NODES - 1), -right[0], 0.0)
    same = (row // 32 == column // 32) & (node == column % 8)
    mixed = jnp.zeros((256, 256), f32)
    for v in range(4):
        for w in range(4):
            mixed = jnp.where(
                ((row // 8) % 4 == v) & ((column // 8) % 4 == w), mixing[comp, v, w], mixed
            )
    across += jnp.where(same, mixed, 0.0)
    across_high, across_low = split(across)

    for ey in range(EY):
        lines = [y_row(field, ey * 8 + j) for j in range(8)]
        stacked = jnp.concatenate(lines, axis=0)
        stacked_high, stacked_low = split(stacked)
        rate = dot(jnp.concatenate([stacked_high, stacked_low], axis=1), z_high)
        rate += dot(stacked_high, z_low)
        pair = dot(across_high, jnp.concatenate([stacked_high, stacked_low], axis=1))
        rate += pair[:, :128] + pair[:, 128:] + dot(across_low, stacked_high)
        along_y = []
        for m in range(8):
            total = float(derivative[m, 0]) * lines[0]
            for j in range(1, 8):
                total += float(derivative[m, j]) * lines[j]
            total = -speed[1] * total
            if m == 0:
                total -= left[1] * lines[0]
                if ey > 0:
                    total += left[1] * y_row(field, ey * 8 - 1)
            if m == NODES - 1:
                total -= right[1] * lines[m]
                if ey < EY - 1:
                    total += right[1] * y_row(field, ey * 8 + 8)
            along_y.append(total)
        rate += jnp.concatenate(along_y, axis=0)
        kept = jnp.concatenate([y_row(register, ey * 8 + j) for j in range(8)], axis=0)
        base[ey * 256 : (ey + 1) * 256, :] = register_keep * kept + time_step * rate


def scattered(slots, message):
    head = message[2 * slots : 2 * slots + 8, 0:slots]
    kind = head[6:7]
    target = jnp.where(kind > 0.0, head[4:5] * 16.0 + head[5:6], -1.0).astype(jnp.int32)
    both = jnp.concatenate([target, target], axis=1)
    placed = one(iota((FACES, 2 * slots), 0) == both)
    values = jnp.concatenate([message[0:slots, :], message[slots : 2 * slots, :]], axis=1)
    high = values.astype(bf16).astype(f32)
    total = dot(placed, jnp.concatenate([high, values - high], axis=0).astype(bf16))
    row = iota((16, 2 * slots), 0)
    quadrant = ((row % 8) // 4) * 2 + row // 8
    kind = jnp.where(iota((1, 2 * slots), 1) < slots, jnp.concatenate([kind, kind], axis=1), 0.0)
    live = (kind == 1.0) | (kind == 2.0 + quadrant.astype(f32))
    return total, dot_t(one(live & (kind > 0.0)), placed)


def early_kernel(slots, *refs):
    *messages, total_out, masks_out = refs
    parts = [scattered(slots, message) for message in messages]
    total_out[...] = sum(part[0] for part in parts)
    masks_out[...] = sum(part[1] for part in parts)


def finish_kernel(late, slots, *refs):
    messages = refs[:late]
    early_total, early_masks, *refs = refs[late:]
    base, field, faces, y_before, y_after, gains = refs[:6]
    layers = refs[6:-5]
    new_out, advanced_out, new, advanced, left = refs[-5:]
    total, masks = early_total[...], early_masks[...]
    for message in messages:
        part, named = scattered(slots, message)
        total += part
        masks += named
    total = total.T
    terms = []
    for v in range(4):
        gain = gains[v : v + 1, 0:1]
        for b in range(8):
            at = (v * 8 + b) * 8
            count = masks[0:8] if b < 4 else masks[8:16]
            terms.append(gain * (total[at : at + 8] - count * faces[at : at + 8, :]))
    turned = []
    for lanes in (slice(0, 128), slice(128, 256)):
        turned += block_transpose(
            [
                jnp.concatenate([terms[v * 8 + b][:, lanes] for v in range(4)], axis=0)
                for b in range(8)
            ]
        )
    high, low = split(jnp.concatenate(turned, axis=0))
    moved = dot(jnp.concatenate([high, low], axis=1), twice(lane_order(True)))
    high, low = split(jnp.concatenate([term[:, 256:384] for term in terms], axis=0))
    ends = jnp.concatenate([end_lanes(ey, True) for ey in range(EY)], axis=1)
    on_z = dot(jnp.concatenate([high, low], axis=1), twice(ends))

    copies = []
    for v in range(4):
        for ey in range(EY):
            for j in range(8):
                y = ey * 8 + j
                at = (v * 8 + j) * 8
                rate = base[y * 32 + v * 8 : y * 32 + v * 8 + 8, :]
                rate += on_z[at : at + 8, ey * 128 : ey * 128 + 128]
                if j in (0, NODES - 1):
                    at = ((8 + (4 if j else 0) + ey) * 4 + v) * 8
                    rate += moved[at : at + 8]
                if y == 0:
                    rate += gains[4:5, :] * y_before[v * 8 : v * 8 + 8, :]
                if y == 31:
                    rate += gains[5:6, :] * y_after[v * 8 : v * 8 + 8, :]
                new[pl.ds(v * 256 + y, 8, stride=32), :] = rate
        for end in (0, 1):
            at = v * 256 + (NODES - 1) * end * 32
            coupled = jnp.concatenate(
                [
                    moved[((end * 4 + ey) * 4 + v) * 8 : ((end * 4 + ey) * 4 + v) * 8 + 8]
                    for ey in range(EY)
                ],
                axis=0,
            )
            for i in range(len(layers)):
                beside = layers[i][v * 32 : v * 32 + 32, :]
                coupled += gains[6 + 2 * i + end : 7 + 2 * i + end, :] * beside
            new[pl.ds(at, 32), :] = new[pl.ds(at, 32), :] + coupled
        rows = pl.ds(v * 256, 256)
        advanced[rows, :] = field[rows, :] + section_weight * new[rows, :]
        for i, (source, place) in enumerate(((new, new_out), (advanced, advanced_out))):
            copies.append(
                pltpu.make_async_copy(source.at[rows], place.at[rows], left.at[v * 2 + i])
            )
            copies[-1].start()
    for copy in copies:
        copy.wait()


def along(layer, axis, step):
    devices = lax.axis_size(axis)
    pairs = [(i, i + step) for i in range(devices) if 0 <= i + step < devices]
    return lax.ppermute(layer, axis, pairs)


def on_device(
    field, register, advect, mixing, drag, face_elem, face_side, mortar_code, partner_rank,
    partner_elem, partner_side, partner_quadrant, face_count,
):
    ranks = lax.axis_size("elem")
    capacity = face_elem.shape[-1]
    slots = max(2, 2 * capacity // ranks)
    subs = lax.axis_size("sub")
    layers = 1 if subs == 2 else 2
    carriers = neighbour_messages(ranks)
    flat = field.reshape(1024, 128)
    vmem = pl.BlockSpec(memory_space=pltpu.VMEM)
    smem = pl.BlockSpec(memory_space=pltpu.SMEM)
    row = (1, capacity)
    plan = pl.pallas_call(
        functools.partial(plan_kernel, ranks, slots),
        out_shape=[
            jax.ShapeDtypeStruct((8, capacity), f32),
            jax.ShapeDtypeStruct((capacity, 1), f32),
            jax.ShapeDtypeStruct((capacity, FACES), bf16),
            jax.ShapeDtypeStruct((ranks * slots, capacity), bf16),
            jax.ShapeDtypeStruct((256, CODES * 64), bf16),
        ],
        in_specs=[vmem] * 7,
        out_specs=[vmem] * 5,
        compiler_params=pltpu.CompilerParams(vmem_limit_bytes=32 << 20),
        cost_estimate=pl.CostEstimate(flops=10**9, bytes_accessed=8 << 20, transcendentals=0),
        name="plan_records",
    )(
        face_elem.reshape(row), face_side.reshape(row), mortar_code.reshape(row),
        partner_rank.reshape(row), partner_elem.reshape(row), partner_side.reshape(row),
        partner_quadrant.reshape(row),
    )
    face_count, plan = lax.optimization_barrier((face_count, plan))
    outs = pl.pallas_call(
        functools.partial(send_kernel, ranks, slots),
        out_shape=[jax.ShapeDtypeStruct((2 * slots + 8, 128), f32)] * ranks
        + [jax.ShapeDtypeStruct((256, FACES), f32)],
        in_specs=[vmem] * 7,
        out_specs=[vmem] * (ranks + 1),
        compiler_params=pltpu.CompilerParams(vmem_limit_bytes=32 << 20),
        cost_estimate=pl.CostEstimate(flops=10**8, bytes_accessed=2 << 20, transcendentals=0),
        name="send_faces",
    )(flat, face_count.reshape(1, 1), *plan)
    faces = outs[ranks]
    outgoing = dict(zip(send_order(ranks), outs))
    received = {}
    for k in send_order(ranks):
        pairs = [(2 * e + c, 2 * (e ^ k) + 1 - c) for e in range(ranks) for c in range(2)]
        received[k] = lax.ppermute(outgoing[k], ("elem", "comp"), pairs)

    layers_out = pl.pallas_call(
        functools.partial(layers_kernel, ranks),
        out_shape=[jax.ShapeDtypeStruct((128, 128), f32)] * len(carriers)
        + [jax.ShapeDtypeStruct((32, 128), f32)] * layers,
        in_specs=[vmem, pl.BlockSpec(memory_space=pl.ANY)],
        out_specs=[vmem] * (len(carriers) + layers),
        compiler_params=pltpu.CompilerParams(vmem_limit_bytes=8 << 20),
        cost_estimate=pl.CostEstimate(flops=10**4, bytes_accessed=1 << 18, transcendentals=0),
        name="halo_layers",
    )(flat, received[0])
    x_layers, y_layers = layers_out[: len(carriers)], layers_out[len(carriers) :]
    beside = []
    for k, layer in zip(carriers, x_layers):
        pairs = [(e, e ^ k) for e in range(ranks) if abs((e ^ k) - e) == 1]
        beside.append(lax.ppermute(layer, "elem", pairs))
    if layers == 1:
        y_before = y_after = lax.ppermute(y_layers[0], "sub", [(0, 1), (1, 0)])
    else:
        y_before = along(y_layers[1], "sub", 1)
        y_after = along(y_layers[0], "sub", -1)
    base, gains = pl.pallas_call(
        functools.partial(local_kernel, ranks),
        out_shape=[
            jax.ShapeDtypeStruct((1024, 128), f32),
            jax.ShapeDtypeStruct((16, 128), f32),
        ],
        in_specs=[vmem, vmem, smem, smem, smem, pl.BlockSpec(memory_space=pl.ANY)],
        out_specs=[vmem] * 2,
        compiler_params=pltpu.CompilerParams(vmem_limit_bytes=32 << 20),
        cost_estimate=pl.CostEstimate(flops=5 * 10**8, bytes_accessed=4 << 20, transcendentals=0),
        name="local_rate",
    )(
        flat, register.reshape(1024, 128), advect, mixing, drag, received[0],
    )
    order = send_order(ranks)
    early, late = order[: len(carriers)] + order[-1:], order[len(carriers) : -1]
    sums = pl.pallas_call(
        functools.partial(early_kernel, slots),
        out_shape=[jax.ShapeDtypeStruct((FACES, 256), f32), jax.ShapeDtypeStruct((16, FACES), f32)],
        in_specs=[vmem] * len(early),
        out_specs=[vmem] * 2,
        compiler_params=pltpu.CompilerParams(vmem_limit_bytes=16 << 20),
        cost_estimate=pl.CostEstimate(flops=10**6, bytes_accessed=1 << 18, transcendentals=0),
        name="early_sums",
    )(*[received[k] for k in early])
    new, advanced = pl.pallas_call(
        functools.partial(finish_kernel, len(late), slots),
        out_shape=[jax.ShapeDtypeStruct((1024, 128), f32)] * 2,
        in_specs=[vmem] * (len(late) + 8 + len(carriers)),
        out_specs=[pl.BlockSpec(memory_space=pl.ANY)] * 2,
        scratch_shapes=[pltpu.VMEM((1024, 128), f32)] * 2 + [pltpu.SemaphoreType.DMA((8,))],
        compiler_params=pltpu.CompilerParams(vmem_limit_bytes=32 << 20),
        cost_estimate=pl.CostEstimate(flops=10**8, bytes_accessed=4 << 20, transcendentals=0),
        name="couple_and_finish",
    )(
        *[received[k] for k in late], *sums, base, flat, faces, y_before, y_after, gains, *beside
    )
    return new.reshape(field.shape), advanced.reshape(field.shape)


def solution(mesh):
    block = P("comp", None, ("parts", "elem"), "sub", None)
    records = P("comp", ("parts", "elem"), "sub", None)
    in_specs = (
        block, block, P(), P(), P(), records, records, records,
        P("comp", ("parts", "elem"), "sub", None, None), records, records, records,
        P("comp", ("parts", "elem"), "sub"),
    )
    return jax.shard_map(
        on_device, mesh=mesh, in_specs=in_specs, out_specs=(block, block), check_vma=False
    )
```

```python
import functools
import math

import jax
import jax.numpy as jnp
import numpy as np
from jax import lax
from jax.experimental import pallas as pl
from jax.experimental.pallas import tpu as pltpu
from jax.sharding import PartitionSpec as P

NODES = 8
EY = 4
EZ = 16
FACES = 384
CODES = 8

upwind_share = 0.5
register_keep = -0.4178904745
section_weight = 1.7201463215
time_step = 0.05

f32 = jnp.float32
bf16 = jnp.bfloat16


def legendre_values(point, count):
    values = [1.0, point]
    for power in range(2, count):
        values.append(
            ((2 * power - 1) * point * values[power - 1] - (power - 1) * values[power - 2]) / power
        )
    return values[:count]


def lagrange_rows(points, targets):
    total = len(points)
    result = np.ones((len(targets), total))
    for row, target in enumerate(targets):
        for column in range(total):
            for other in range(total):
                if other != column:
                    result[row, column] *= (target - points[other]) / (
                        points[column] - points[other]
                    )
    return result


@functools.lru_cache
def node_tables(nodes):
    degree = nodes - 1
    guesses = [math.cos(math.pi * position / degree) for position in range(nodes)]
    for sweep in range(100):
        updated = []
        for point in guesses:
            values = legendre_values(point, nodes)
            updated.append(
                point - (point * values[degree] - values[degree - 1]) / (nodes * values[degree])
            )
        guesses = updated
    points = sorted(guesses)
    points[0] = -1.0
    points[-1] = 1.0
    basis = np.array([legendre_values(point, nodes) for point in points])
    inverse = np.linalg.inv(basis)
    barycentric = []
    for position in range(nodes):
        product = 1.0
        for other in range(nodes):
            if other != position:
                product = product * (points[position] - points[other])
        barycentric.append(1.0 / product)
    derivative = np.zeros((nodes, nodes))
    for position in range(nodes):
        for other in range(nodes):
            if other != position:
                derivative[position, other] = (
                    barycentric[other] / barycentric[position] / (points[position] - points[other])
                )
        derivative[position, position] = -derivative[position].sum()
    mask = np.array([[point < 0 for point in points], [point > 0 for point in points]], np.float64)
    fine = [lagrange_rows(points, [(point + shift) / 2.0 for point in points]) for shift in (-1, 1)]
    coarse = []
    for half, shift in ((0, 1.0), (1, -1.0)):
        values = np.array([legendre_values(2.0 * point + shift, nodes) for point in points])
        coarse.append((values * mask[half][:, None]) @ inverse)
    return derivative, degree * nodes / 2.0, fine, coarse


def split(values):
    high = values.astype(bf16)
    return high, (values - high.astype(f32)).astype(bf16)


def dot(left, right):
    return lax.dot_general(left, right, (((1,), (0,)), ((), ())), preferred_element_type=f32)


def dot_t(left, right):
    return lax.dot_general(left, right, (((1,), (1,)), ((), ())), preferred_element_type=f32)


def iota(shape, dim):
    return lax.broadcasted_iota(jnp.int32, shape, dim)


def one(condition):
    return jnp.where(condition, 1.0, 0.0).astype(bf16)


def twice(matrix):
    return jnp.concatenate([matrix, matrix], axis=0)


def block_transpose(parts):
    parts = list(parts)
    block = iota(parts[0].shape, 1) // 16
    for bit in (1, 2, 4):
        upper = (block & bit) != 0
        for g in range(8):
            if g & bit:
                continue
            low, high = parts[g], parts[g | bit]
            parts[g] = jnp.where(upper, pltpu.roll(high, 16 * bit, 1), low)
            parts[g | bit] = jnp.where(upper, high, pltpu.roll(low, 128 - 16 * bit, 1))
    return parts


def lane_order(inverse):
    row, column = iota((128, 128), 1 if inverse else 0), iota((128, 128), 0 if inverse else 1)
    return one(((row // 8) == (column % 16)) & ((row % 8) == (column // 16)))


def end_lanes(ey, inverse):
    z, lane = iota((128, 128), 1 if inverse else 0), iota((128, 128), 0 if inverse else 1)
    return one(
        (lane // 32 == ey) & (z // 8 == lane % 16) & (z % 8 == (NODES - 1) * ((lane // 16) % 2))
    )


def table_tiles(tables, node):
    place = iota((8, 128), 0) * 8 + node
    tiles = [jnp.zeros((8, 128), f32) for _ in tables]
    for i in range(8):
        for j in range(8):
            here = place == i * 8 + j
            tiles = [
                jnp.where(here, float(table[j, i]), tile) for table, tile in zip(tables, tiles)
            ]
    return tiles


def y_row(ref, y):
    return ref[pl.ds(y, 32, stride=32), :]


def face_number(elem, side):
    direction, end = side >> 1, side & 1
    ey, ez = elem >> 4, elem & 15
    group = jnp.where(direction == 2, 16 + 2 * ey + end, direction * 8 + end * 4 + ey)
    return group, ez


def send_order(ranks):
    near = neighbour_messages(ranks)[::-1]
    return near + [k for k in range(1, ranks)[::-1] if k not in near] + [0]


def neighbour_messages(ranks):
    return [k for k in range(1, ranks) if k & (k + 1) == 0]


def plan_kernel(
    ranks, slots, elem, side, code, rank, p_elem, p_side, p_quadrant,
    head_out, which_out, picked_out, placed_out, maps, order_out, ends_out, back_out, ends_back_out,
):
    order_out[...] = twice(lane_order(False))
    for ey in range(EY):
        ends_out[ey * 256 : ey * 256 + 256, :] = twice(end_lanes(ey, False))
        ends_back_out[:, ey * 128 : ey * 128 + 128] = twice(end_lanes(ey, True))
    back_out[...] = twice(lane_order(True))
    capacity = elem.shape[1]
    me = lax.axis_index("elem")
    group, ez = face_number(elem[...], side[...])
    codes = code[...]
    map_index = jnp.where(codes == 5, 5 + p_quadrant[...], codes)
    apart = rank[...] ^ me
    to_group, to_ez = face_number(p_elem[...], p_side[...])
    kind = jnp.where(codes == 5, 2 + p_quadrant[...], 1)
    rows = [group, ez, map_index, apart, to_group, to_ez, kind]
    head = jnp.concatenate(
        [row.astype(f32) for row in rows] + [jnp.zeros((1, capacity), f32)], axis=0
    )
    head_out[...] = head
    here, there = iota((capacity, capacity), 0), iota((capacity, capacity), 1)
    columns = dot_t(one(here == there), head.astype(bf16))
    which_out[...] = columns[:, 2:3]
    source = (columns[:, 0:1] * 16.0 + columns[:, 1:2]).astype(jnp.int32)
    picked_out[...] = one(source == iota((capacity, FACES), 1))
    earlier = (columns[:, 3:4] == apart.astype(f32)) & (here < there)
    position = jnp.sum(jnp.where(earlier, 1.0, 0.0), axis=0, keepdims=True).astype(jnp.int32)
    slot = jnp.where(position < slots, apart * slots + position, -1)
    placed_out[...] = one(iota((ranks * slots, capacity), 0) == slot)

    _, _, fine, coarse = node_tables(NODES)
    lane = iota((8, 128), 1)
    along_a = table_tiles(fine + coarse, lane % 8)
    along_b = table_tiles(fine + coarse, lane // 8 % 8)
    lower = lane < 64
    for pair in range(CODES // 2):
        tiles = []
        for index in (2 * pair, 2 * pair + 1):
            tiles.append(
                (along_a[index // 4 * 2 + index % 4 // 2], along_b[index // 4 * 2 + index % 2])
            )
        first = jnp.where(lower, tiles[0][0], tiles[1][0])
        second = jnp.where(lower, tiles[0][1], tiles[1][1])
        high, low = split(
            jnp.concatenate([first * second[b : b + 1, :] for b in range(8)], axis=0)
        )
        lanes = slice(pair * 128, pair * 128 + 128)
        maps[0:64, lanes] = high
        maps[64:128, lanes] = high
        maps[128:192, lanes] = low
        maps[192:256, lanes] = jnp.zeros((64, 128), bf16)


def send_kernel(
    ranks, slots, field, count, planned, which_in, picked, placed_in, maps, order, ends_of, *outs
):
    messages, faces_out = outs[:ranks], outs[ranks]
    capacity = planned.shape[1]
    lines = iota((8, capacity), 0)
    unused = (lines == 6) & (iota((8, capacity), 1) >= count[...])
    head = jnp.where(unused, 0.0, planned[...]).astype(bf16)
    parts = []
    for kind_of in (0, 1):
        blocks = []
        for end in (0, 1):
            for ey in range(EY):
                if kind_of == 0:
                    blocks += [
                        field[pl.ds(v * 256 + (NODES - 1) * end * 32 + ey * 8, 8), :]
                        for v in range(4)
                    ]
                else:
                    blocks.append(y_row(field, ey * 8 + (NODES - 1) * end))
        stacked_high, stacked_low = split(jnp.concatenate(blocks, axis=0))
        moved = dot(jnp.concatenate([stacked_high, stacked_low], axis=1), order[...])
        turned = block_transpose([moved[g * 32 : (g + 1) * 32] for g in range(8)])
        parts.append(
            jnp.concatenate(
                [turned[b][v * 8 : (v + 1) * 8] for v in range(4) for b in range(8)], axis=0
            )
        )
    stacks = []
    for ey in range(EY):
        lines = [y_row(field, ey * 8 + b) for b in range(8)]
        stacks += split(
            jnp.concatenate(
                [lines[b][v * 8 : (v + 1) * 8] for v in range(4) for b in range(8)], axis=0
            )
        )
    ends = dot(jnp.concatenate(stacks, axis=1), ends_of[...])
    parts.append(ends)
    faces = jnp.concatenate(parts, axis=1)
    faces_out[...] = faces

    faces_high, faces_low = split(faces)
    values = dot_t(
        jnp.concatenate([picked[...], picked[...]], axis=1),
        jnp.concatenate([faces_high, faces_low], axis=1),
    )
    lower = iota((capacity, 128), 1) < 64
    halves = [values[:, :128], values[:, 128:]]
    stacked = []
    for half in halves:
        crossed = pltpu.roll(half, 64, 1)
        high, crossed_high = [part.astype(bf16).astype(f32) for part in (half, crossed)]
        low, crossed_low = half - high, crossed - crossed_high
        stacked.append(jnp.concatenate([jnp.where(lower, high, crossed_low), high], axis=1))
        stacked.append(
            jnp.concatenate([jnp.where(lower, crossed_high, low), crossed_high], axis=1)
        )
    out = dot(jnp.concatenate(stacked, axis=0).astype(bf16), maps[...])
    which = which_in[...].astype(jnp.int32)
    column, odd = (which - 1) >> 1, (which - 1) & 1
    mapped = []
    for h, half in enumerate(halves):
        sides = []
        for v in (2 * h, 2 * h + 1):
            rows = out[v * capacity : (v + 1) * capacity]
            taken = rows[:, :128]
            for pair in range(1, CODES // 2):
                taken = jnp.where(column == pair, rows[:, pair * 128 : pair * 128 + 128], taken)
            sides.append(jnp.where(odd == v % 2, taken, pltpu.roll(taken, 64, 1)))
        mapped.append(jnp.where(which == 0, half, jnp.where(lower, sides[0], sides[1])))
    mapped_high, mapped_low = split(jnp.concatenate(mapped, axis=1))
    rows = dot(placed_in[...], mapped_high) + dot(placed_in[...], mapped_low)
    heads = dot_t(head, placed_in[...])
    for message, k in zip(messages, send_order(ranks)):
        here = slice(k * slots, (k + 1) * slots)
        message[0:slots, :] = rows[here, :128]
        message[slots : 2 * slots, :] = rows[here, 128:]
        message[2 * slots : 2 * slots + 8, :] = jnp.zeros((8, 128), f32)
        message[2 * slots : 2 * slots + 8, 0:slots] = heads[:, here]


def layers_kernel(ranks, field, after, *outs):
    carriers = len(neighbour_messages(ranks))
    x_layers, y_layers = outs[:carriers], outs[carriers:]
    me = lax.axis_index("elem")
    for i, k in enumerate(neighbour_messages(ranks)):
        for v in range(4):
            x_layers[i][v * 32 : v * 32 + 32, :] = jnp.where(
                me ^ k == me + 1,
                field[v * 256 + 224 : v * 256 + 256, :],
                field[v * 256 : v * 256 + 32, :],
            )
    if len(y_layers) == 1:
        y_layers[0][...] = jnp.where(lax.axis_index("sub") == 0, y_row(field, 31), y_row(field, 0))
    else:
        y_layers[0][...] = y_row(field, 0)
        y_layers[1][...] = y_row(field, 31)


def local_kernel(
    ranks, field, register, advect, mixing, drag, after, base, gains
):
    comp = lax.axis_index("comp")
    derivative, scale, _, _ = node_tables(NODES)
    left, right, speed = [], [], []
    for d in range(3):
        a = advect[comp, d]
        speed.append(a)
        left.append(scale * (0.5 * a + 0.5 * upwind_share * jnp.abs(a)))
        right.append(scale * (0.5 * upwind_share * jnp.abs(a) - 0.5 * a))

    me, sub, subs = lax.axis_index("elem"), lax.axis_index("sub"), lax.axis_size("sub")
    values = [drag[comp, v] * scale for v in range(4)]
    values.append(jnp.where(sub > 0, left[1], 0.0))
    values.append(jnp.where(sub < subs - 1, right[1], 0.0))
    for k in neighbour_messages(ranks):
        values.append(jnp.where(me ^ k == me - 1, left[0], 0.0))
        values.append(jnp.where(me ^ k == me + 1, right[0], 0.0))
    line = iota(gains.shape, 0)
    lines = jnp.zeros(gains.shape, f32)
    for i, value in enumerate(values):
        lines = jnp.where(line == i, time_step * value, lines)
    gains[...] = lines
    tile_z, tile_y = table_tiles([derivative, derivative.T], iota((8, 128), 1) % 8)

    def both_ways(row, column, node, gain_left, gain_right):
        first, last = node == 0, node == NODES - 1
        out = jnp.where((row == column) & first, -gain_left, 0.0)
        out = jnp.where((row == column) & last, -gain_right, out)
        out = jnp.where((row == column - 1) & first, gain_left, out)
        return jnp.where((row == column + 1) & last, gain_right, out)

    row, column = iota((128, 128), 0), iota((128, 128), 1)
    along_z = both_ways(row, column, column % 8, left[2], right[2]) - speed[2] * jnp.where(
        row // 8 == column // 8, jnp.concatenate([tile_z] * 16, axis=0), 0.0
    )
    z_high, z_low = split(along_z)
    z_high = twice(z_high)
    row, column = iota((256, 256), 0), iota((256, 256), 1)
    node = row % 8
    tile = jnp.concatenate([tile_y] * 2, axis=1)
    across = jnp.where(
        row // 8 == column // 8, -speed[0] * jnp.concatenate([tile] * 32, axis=0), 0.0
    )
    across += jnp.where((row == column) & (node == 0), -left[0], 0.0)
    across += jnp.where((row == column) & (node == NODES - 1), -right[0], 0.0)
    same = (row // 32 == column // 32) & (node == column % 8)
    mixed = jnp.zeros((256, 256), f32)
    for v in range(4):
        for w in range(4):
            mixed = jnp.where(
                ((row // 8) % 4 == v) & ((column // 8) % 4 == w), mixing[comp, v, w], mixed
            )
    across += jnp.where(same, mixed, 0.0)
    across_high, across_low = split(across)

    for ey in range(EY):
        lines = [y_row(field, ey * 8 + j) for j in range(8)]
        stacked = jnp.concatenate(lines, axis=0)
        stacked_high, stacked_low = split(stacked)
        rate = dot(jnp.concatenate([stacked_high, stacked_low], axis=1), z_high)
        rate += dot(stacked_high, z_low)
        pair = dot(across_high, jnp.concatenate([stacked_high, stacked_low], axis=1))
        rate += pair[:, :128] + pair[:, 128:] + dot(across_low, stacked_high)
        along_y = []
        for m in range(8):
            total = float(derivative[m, 0]) * lines[0]
            for j in range(1, 8):
                total += float(derivative[m, j]) * lines[j]
            total = -speed[1] * total
            if m == 0:
                total -= left[1] * lines[0]
                if ey > 0:
                    total += left[1] * y_row(field, ey * 8 - 1)
            if m == NODES - 1:
                total -= right[1] * lines[m]
                if ey < EY - 1:
                    total += right[1] * y_row(field, ey * 8 + 8)
            along_y.append(total)
        rate += jnp.concatenate(along_y, axis=0)
        kept = jnp.concatenate([y_row(register, ey * 8 + j) for j in range(8)], axis=0)
        base[ey * 256 : (ey + 1) * 256, :] = register_keep * kept + time_step * rate


def scattered(slots, message):
    head = message[2 * slots : 2 * slots + 8, 0:slots]
    kind = head[6:7]
    target = jnp.where(kind > 0.0, head[4:5] * 16.0 + head[5:6], -1.0).astype(jnp.int32)
    both = jnp.concatenate([target, target], axis=1)
    placed = one(iota((FACES, 2 * slots), 0) == both)
    values = jnp.concatenate([message[0:slots, :], message[slots : 2 * slots, :]], axis=1)
    high = values.astype(bf16).astype(f32)
    total = dot(placed, jnp.concatenate([high, values - high], axis=0).astype(bf16))
    row = iota((16, 2 * slots), 0)
    quadrant = ((row % 8) // 4) * 2 + row // 8
    kind = jnp.where(iota((1, 2 * slots), 1) < slots, jnp.concatenate([kind, kind], axis=1), 0.0)
    live = (kind == 1.0) | (kind == 2.0 + quadrant.astype(f32))
    return total, dot_t(one(live & (kind > 0.0)), placed)


def early_kernel(slots, *refs):
    *messages, total_out, masks_out = refs
    parts = [scattered(slots, message) for message in messages]
    total_out[...] = sum(part[0] for part in parts)
    masks_out[...] = sum(part[1] for part in parts)


def finish_kernel(late, slots, *refs):
    messages = refs[:late]
    early_total, early_masks, *refs = refs[late:]
    base, field, faces, y_before, y_after, gains, back, ends_back = refs[:8]
    layers = refs[8:-5]
    new_out, advanced_out, new, advanced, left = refs[-5:]
    total, masks = early_total[...], early_masks[...]
    for message in messages:
        part, named = scattered(slots, message)
        total += part
        masks += named
    total = total.T
    terms = []
    for v in range(4):
        gain = gains[v : v + 1, 0:1]
        for b in range(8):
            at = (v * 8 + b) * 8
            count = masks[0:8] if b < 4 else masks[8:16]
            terms.append(gain * (total[at : at + 8] - count * faces[at : at + 8, :]))
    turned = []
    for lanes in (slice(0, 128), slice(128, 256)):
        turned += block_transpose(
            [
                jnp.concatenate([terms[v * 8 + b][:, lanes] for v in range(4)], axis=0)
                for b in range(8)
            ]
        )
    high, low = split(jnp.concatenate(turned, axis=0))
    moved = dot(jnp.concatenate([high, low], axis=1), back[...])
    high, low = split(jnp.concatenate([term[:, 256:384] for term in terms], axis=0))
    on_z = dot(jnp.concatenate([high, low], axis=1), ends_back[...])

    copies = []
    for v in range(4):
        for ey in range(EY):
            for j in range(8):
                y = ey * 8 + j
                at = (v * 8 + j) * 8
                rate = base[y * 32 + v * 8 : y * 32 + v * 8 + 8, :]
                rate += on_z[at : at + 8, ey * 128 : ey * 128 + 128]
                if j in (0, NODES - 1):
                    at = ((8 + (4 if j else 0) + ey) * 4 + v) * 8
                    rate += moved[at : at + 8]
                if y == 0:
                    rate += gains[4:5, :] * y_before[v * 8 : v * 8 + 8, :]
                if y == 31:
                    rate += gains[5:6, :] * y_after[v * 8 : v * 8 + 8, :]
                new[pl.ds(v * 256 + y, 8, stride=32), :] = rate
        for end in (0, 1):
            at = v * 256 + (NODES - 1) * end * 32
            coupled = jnp.concatenate(
                [
                    moved[((end * 4 + ey) * 4 + v) * 8 : ((end * 4 + ey) * 4 + v) * 8 + 8]
                    for ey in range(EY)
                ],
                axis=0,
            )
            for i in range(len(layers)):
                beside = layers[i][v * 32 : v * 32 + 32, :]
                coupled += gains[6 + 2 * i + end : 7 + 2 * i + end, :] * beside
            new[pl.ds(at, 32), :] = new[pl.ds(at, 32), :] + coupled
        rows = pl.ds(v * 256, 256)
        advanced[rows, :] = field[rows, :] + section_weight * new[rows, :]
        for i, (source, place) in enumerate(((new, new_out), (advanced, advanced_out))):
            copies.append(
                pltpu.make_async_copy(source.at[rows], place.at[rows], left.at[v * 2 + i])
            )
            copies[-1].start()
    for copy in copies:
        copy.wait()


def along(layer, axis, step):
    devices = lax.axis_size(axis)
    pairs = [(i, i + step) for i in range(devices) if 0 <= i + step < devices]
    return lax.ppermute(layer, axis, pairs)


def on_device(
    field, register, advect, mixing, drag, face_elem, face_side, mortar_code, partner_rank,
    partner_elem, partner_side, partner_quadrant, face_count,
):
    ranks = lax.axis_size("elem")
    capacity = face_elem.shape[-1]
    slots = max(2, 2 * capacity // ranks)
    subs = lax.axis_size("sub")
    layers = 1 if subs == 2 else 2
    carriers = neighbour_messages(ranks)
    flat = field.reshape(1024, 128)
    vmem = pl.BlockSpec(memory_space=pltpu.VMEM)
    smem = pl.BlockSpec(memory_space=pltpu.SMEM)
    row = (1, capacity)
    plan = pl.pallas_call(
        functools.partial(plan_kernel, ranks, slots),
        out_shape=[
            jax.ShapeDtypeStruct((8, capacity), f32),
            jax.ShapeDtypeStruct((capacity, 1), f32),
            jax.ShapeDtypeStruct((capacity, FACES), bf16),
            jax.ShapeDtypeStruct((ranks * slots, capacity), bf16),
            jax.ShapeDtypeStruct((256, CODES * 64), bf16),
            jax.ShapeDtypeStruct((256, 128), bf16),
            jax.ShapeDtypeStruct((EY * 256, 128), bf16),
            jax.ShapeDtypeStruct((256, 128), bf16),
            jax.ShapeDtypeStruct((256, EY * 128), bf16),
        ],
        in_specs=[vmem] * 7,
        out_specs=[vmem] * 9,
        compiler_params=pltpu.CompilerParams(vmem_limit_bytes=32 << 20),
        cost_estimate=pl.CostEstimate(flops=10**9, bytes_accessed=8 << 20, transcendentals=0),
        name="plan_records",
    )(
        face_elem.reshape(row), face_side.reshape(row), mortar_code.reshape(row),
        partner_rank.reshape(row), partner_elem.reshape(row), partner_side.reshape(row),
        partner_quadrant.reshape(row),
    )
    face_count, plan = lax.optimization_barrier((face_count, plan))
    outs = pl.pallas_call(
        functools.partial(send_kernel, ranks, slots),
        out_shape=[jax.ShapeDtypeStruct((2 * slots + 8, 128), f32)] * ranks
        + [jax.ShapeDtypeStruct((256, FACES), f32)],
        in_specs=[vmem] * 9,
        out_specs=[vmem] * (ranks + 1),
        compiler_params=pltpu.CompilerParams(vmem_limit_bytes=32 << 20),
        cost_estimate=pl.CostEstimate(flops=10**8, bytes_accessed=2 << 20, transcendentals=0),
        name="send_faces",
    )(flat, face_count.reshape(1, 1), *plan[:-2])
    faces = outs[ranks]
    outgoing = dict(zip(send_order(ranks), outs))
    received = {}
    for k in send_order(ranks):
        pairs = [(2 * e + c, 2 * (e ^ k) + 1 - c) for e in range(ranks) for c in range(2)]
        received[k] = lax.ppermute(outgoing[k], ("elem", "comp"), pairs)

    layers_out = pl.pallas_call(
        functools.partial(layers_kernel, ranks),
        out_shape=[jax.ShapeDtypeStruct((128, 128), f32)] * len(carriers)
        + [jax.ShapeDtypeStruct((32, 128), f32)] * layers,
        in_specs=[vmem, pl.BlockSpec(memory_space=pl.ANY)],
        out_specs=[vmem] * (len(carriers) + layers),
        compiler_params=pltpu.CompilerParams(vmem_limit_bytes=8 << 20),
        cost_estimate=pl.CostEstimate(flops=10**4, bytes_accessed=1 << 18, transcendentals=0),
        name="halo_layers",
    )(flat, received[0])
    x_layers, y_layers = layers_out[: len(carriers)], layers_out[len(carriers) :]
    beside = []
    for k, layer in zip(carriers, x_layers):
        pairs = [(e, e ^ k) for e in range(ranks) if abs((e ^ k) - e) == 1]
        beside.append(lax.ppermute(layer, "elem", pairs))
    if layers == 1:
        y_before = y_after = lax.ppermute(y_layers[0], "sub", [(0, 1), (1, 0)])
    else:
        y_before = along(y_layers[1], "sub", 1)
        y_after = along(y_layers[0], "sub", -1)
    base, gains = pl.pallas_call(
        functools.partial(local_kernel, ranks),
        out_shape=[
            jax.ShapeDtypeStruct((1024, 128), f32),
            jax.ShapeDtypeStruct((16, 128), f32),
        ],
        in_specs=[vmem, vmem, smem, smem, smem, pl.BlockSpec(memory_space=pl.ANY)],
        out_specs=[vmem] * 2,
        compiler_params=pltpu.CompilerParams(vmem_limit_bytes=32 << 20),
        cost_estimate=pl.CostEstimate(flops=5 * 10**8, bytes_accessed=4 << 20, transcendentals=0),
        name="local_rate",
    )(
        flat, register.reshape(1024, 128), advect, mixing, drag, received[0],
    )
    order = send_order(ranks)
    early, late = order[: len(carriers)] + order[-1:], order[len(carriers) : -1]
    sums = pl.pallas_call(
        functools.partial(early_kernel, slots),
        out_shape=[jax.ShapeDtypeStruct((FACES, 256), f32), jax.ShapeDtypeStruct((16, FACES), f32)],
        in_specs=[vmem] * len(early),
        out_specs=[vmem] * 2,
        compiler_params=pltpu.CompilerParams(vmem_limit_bytes=16 << 20),
        cost_estimate=pl.CostEstimate(flops=10**6, bytes_accessed=1 << 18, transcendentals=0),
        name="early_sums",
    )(*[received[k] for k in early])
    new, advanced = pl.pallas_call(
        functools.partial(finish_kernel, len(late), slots),
        out_shape=[jax.ShapeDtypeStruct((1024, 128), f32)] * 2,
        in_specs=[vmem] * (len(late) + 10 + len(carriers)),
        out_specs=[pl.BlockSpec(memory_space=pl.ANY)] * 2,
        scratch_shapes=[pltpu.VMEM((1024, 128), f32)] * 2 + [pltpu.SemaphoreType.DMA((8,))],
        compiler_params=pltpu.CompilerParams(vmem_limit_bytes=32 << 20),
        cost_estimate=pl.CostEstimate(flops=10**8, bytes_accessed=4 << 20, transcendentals=0),
        name="couple_and_finish",
    )(
        *[received[k] for k in late], *sums, base, flat, faces, y_before, y_after, gains, *plan[-2:], *beside
    )
    return new.reshape(field.shape), advanced.reshape(field.shape)


def solution(mesh):
    block = P("comp", None, ("parts", "elem"), "sub", None)
    records = P("comp", ("parts", "elem"), "sub", None)
    in_specs = (
        block, block, P(), P(), P(), records, records, records,
        P("comp", ("parts", "elem"), "sub", None, None), records, records, records,
        P("comp", ("parts", "elem"), "sub"),
    )
    return jax.shard_map(
        on_device, mesh=mesh, in_specs=in_specs, out_specs=(block, block), check_vma=False
    )
```
